768 devices in a mesh: intra: 16 (over y_hi, x), inter: 48 (over z, y_lo, core).
Axes of the slice: x: 4, y: 8 (y_hi: 4, y_lo: 2; y = y_hi * 2 + y_lo), z: 12, core: 2. Of those that a mesh axis runs over, the one named last changes fastest.
Arguments:
- tokens: bfloat16 [196608, 4096], P(('intra', 'inter')), may hold values from -6 to 6
- gain: bfloat16 [4096], replicated, may hold values from 0.099609375 to 1.8984375
- codes: bfloat16 [528, 4096], P('inter', 'intra'), may hold values from -127 to 127, as said below
- scales: bfloat16 [528, 32], P('inter', 'intra'), may hold values from 4.9829483e-05 to 0.00049972534
- cotangent: bfloat16 [196608, 528], P(('intra', 'inter')), may hold values from -12 to 12
Outputs:
- keys: bfloat16 [196608, 528], P(('intra', 'inter'))
- grad_tokens: bfloat16 [196608, 4096], P(('intra', 'inter'))
- grad_weight: float32 [528, 4096], P('inter', 'intra')
The draws below stay inside these ranges and needn't reach their ends.
Inputs may be any that keep to these rules, and one draw needn't show every extreme that they name: `codes`: whole numbers.
All inputs are finite; a program needn't handle non-finite values.
Results may differ from the reference program's by a relative error of at most 0.017.
Values may be sent and summed in bfloat16 or wider, within the bound.
No kernel may reach another device: no remote copies, remote signals or barrier semaphores. Data moves between devices by JAX's collectives and lax.ppermute only.
A program may use at most 64 MiB of HBM per device.

```python
import math
import jax
import jax.numpy as jnp
from jax import lax

D = 4096
OUTW = 528
BLOCK = 128
TOK_DEV = 256
TOKENS = 196608
N_INTRA = 16
N_INTER = 48


def draw_codes(key, part):
    key = jax.random.fold_in(key, 7)
    values = jax.random.randint(key, (OUTW, D), -127, 128)
    return values.astype(jnp.float32).astype(jnp.bfloat16)


def spiked(result, key, source, target, parts, factor):
    def block_of(dim):
        return (jnp.arange(result.shape[dim]) // (result.shape[dim] // parts)).reshape((-1,) + (1,) * (result.ndim - 1 - dim))

    first = jax.random.permutation(key, parts)[block_of(target)]
    far = (block_of(target) + parts // 2) % parts
    return jnp.where((block_of(source) == first) | (block_of(source) == far), factor * result, result)


def level_of(stream_key, dims, pieces, smallest, high):
    loudness = 1.0
    for dim, shards_of in pieces:
        heights = jax.random.uniform(jax.random.fold_in(jax.random.fold_in(stream_key, 6), dim), (shards_of,), jnp.float32, smallest / len(pieces), high / len(pieces))
        loudness = loudness * jnp.repeat(jnp.exp(heights), dims[dim] // shards_of).reshape((-1,) + (1,) * (len(dims) - 1 - dim))
    return loudness


def bell_draw(stream_key, dims, width, most, shards=(), dtype=jnp.bfloat16):
    drawn = width * jax.random.normal(stream_key, dims, jnp.float32)
    if shards:
        drawn = drawn * level_of(stream_key, dims, shards, -0.22, 0.18)
    return jnp.clip(drawn, -most, most).astype(dtype)


def noise_with(rng, extent, scale, reach, shards, heavy, dtype=jnp.bfloat16):
    values = scale * jax.random.normal(rng, extent, jnp.float32)
    if shards:
        values = values * level_of(rng, extent, shards, -0.22, 0.18)
    return jnp.clip(spiked(values, jax.random.fold_in(rng, 3), *heavy), -reach, reach).astype(dtype)


def setup_inputs(seed: int = 0) -> dict:
    streams_of = jax.random.split(jax.random.key(seed), 6)
    tokens = bell_draw(streams_of[0], (TOKENS, D), 1.0, 6.0, ((0, 768),))
    gain = jnp.clip(1.0 + 0.18 * jax.random.normal(streams_of[1], (D,), jnp.float32), 0.099609375, 1.8984375).astype(jnp.bfloat16)
    codes = draw_codes(jax.random.fold_in(streams_of[5], 71), 0)
    scales = jnp.clip(jnp.exp(math.log(0.00049972534) - 2.3054518 * jax.random.uniform(streams_of[3], (OUTW, D // BLOCK), jnp.float32) ** level_of(streams_of[3], (OUTW, D // BLOCK), ((0, 48), (1, 16)), -0.2, 0.2)), 4.982948303222656e-05, 0.00049972534).astype(jnp.bfloat16)
    cotangent = noise_with(streams_of[4], (TOKENS, OUTW), 2.0, 12.0, ((0, 768),), (0, 1, 48, 3.25))
    return {"tokens": tokens, "gain": gain, "codes": codes, "scales": scales, "cotangent": cotangent}


EPS = 1e-05

def normed_rows(values, gain):
    meansq = lax.optimization_barrier(jnp.mean(values * values, axis=-1, keepdims=True))
    return values * lax.rsqrt(meansq + EPS) * gain.astype(jnp.float32)

def reference(tokens, gain, codes, scales, cotangent):
    blocks = D // BLOCK
    weight = (codes.astype(jnp.float32).reshape(OUTW, blocks, BLOCK) * scales.astype(jnp.float32)[:, :, None]).reshape(OUTW, D).astype(jnp.bfloat16)
    count = N_INTRA * N_INTER
    token_blocks = tokens.reshape(count, TOK_DEV, D)
    cot_blocks = cotangent.reshape(count, TOK_DEV, OUTW)

    def step(total, pair):
        values, cot = pair
        normed, back = jax.vjp(lambda v: normed_rows(v, gain), values.astype(jnp.float32))
        hidden = normed.astype(jnp.bfloat16)
        keys = lax.dot_general(hidden, weight, (((1,), (1,)), ((), ())), preferred_element_type=jnp.float32).astype(jnp.bfloat16)
        grad_hidden = jnp.dot(cot, weight, preferred_element_type=jnp.float32)
        grad_tokens = back(grad_hidden)[0].astype(jnp.bfloat16)
        term = lax.dot_general(cot, hidden, (((0,), (0,)), ((), ())), preferred_element_type=jnp.float32).astype(jnp.bfloat16)
        term = lax.optimization_barrier(term)
        return (total + term.astype(jnp.float32), (keys, grad_tokens))
    total, outs = lax.scan(step, jnp.zeros((OUTW, D), jnp.float32), (token_blocks, cot_blocks))
    keys = outs[0].reshape(TOKENS, OUTW)
    grad_tokens = outs[1].reshape(TOKENS, D)
    return (keys, grad_tokens, total / count)
```

```python
import numpy as np
import jax
import jax.numpy as jnp
from jax import lax
from jax.experimental import pallas as pl
from jax.experimental.pallas import tpu as pltpu
from jax.sharding import Mesh, PartitionSpec as P

EPS = 1e-05
COL = 256
VMEM = pl.BlockSpec(memory_space=pltpu.VMEM)
PARAMS = pltpu.CompilerParams(vmem_limit_bytes=48 * 1024 * 1024)


def row_orders(n_z, rows):
    group = -(-n_z * rows // 8) * 8
    grouped = np.full((4 * group, 1), -1, np.int32)
    natural = np.zeros((n_z * 4 * rows, 1), np.int32)
    for z in range(n_z):
        for y in range(2):
            for c in range(2):
                for r in range(rows):
                    o = ((z * 2 + y) * 2 + c) * rows + r
                    p = (c * 2 + y) * group + z * rows + r
                    grouped[p, 0] = o
                    natural[o, 0] = p
    return group, grouped, natural


def pick(index, width):
    lanes = lax.broadcasted_iota(jnp.int32, (index.shape[0], width), 1)
    return jnp.where(lanes == index, 1.0, 0.0).astype(jnp.bfloat16)


def dot(a, b, ca, cb):
    return lax.dot_general(a, b, (((ca,), (cb,)), ((), ())), preferred_element_type=jnp.float32)


def term_kernel(tokens, gain, cot, order, term, cot_grouped, inv):
    feats = tokens.shape[1]
    n_x, half = term.shape[1], term.shape[2]
    total = jnp.zeros((tokens.shape[0], COL), jnp.float32)
    for f in range(0, feats, COL):
        v = tokens[:, f : f + COL].astype(jnp.float32)
        total = total + v * v
    r = lax.rsqrt(jnp.sum(total, axis=1, keepdims=True) / feats + EPS)
    inv[...] = jnp.broadcast_to(r, inv.shape)
    for c in range(2):
        chosen = pick(order[c * half : (c + 1) * half, :], cot.shape[0])
        cot_grouped[c] = dot(chosen, cot[...], 1, 0).astype(jnp.bfloat16)
    for f in range(0, feats, COL):
        v = tokens[:, f : f + COL].astype(jnp.float32)
        hid = (v * r * gain[:, f : f + COL].astype(jnp.float32)).astype(jnp.bfloat16)
        y, x = divmod(f // COL, n_x)
        for c in range(2):
            term[c, x, :, y * COL : (y + 1) * COL] = dot(cot_grouped[c], hid, 1, 0).astype(jnp.bfloat16)


def main_kernel(tokens, gain, cot_grouped, inv, order, w, keys, grad, keys_acc, gh, dots):
    i = pl.program_id(0)
    n_x = pl.num_programs(0)
    toks, feats = tokens.shape
    half = w.shape[2]
    r = inv[:, :1]

    @pl.when(i == 0)
    def _():
        keys_acc[...] = jnp.zeros_like(keys_acc)
        dots[...] = jnp.zeros_like(dots)

    for y in range(w.shape[3] // COL):
        at = pl.ds(pl.multiple_of((y * n_x + i) * COL, COL), COL)
        cols = slice(y * COL, (y + 1) * COL)
        v = tokens[:, at].astype(jnp.float32)
        g = gain[:, at].astype(jnp.float32)
        hid = (v * r * g).astype(jnp.bfloat16)
        for c in range(2):
            keys_acc[c * half : (c + 1) * half, :] += dot(w[0, c, :, cols], hid, 1, 1)
        part = dot(cot_grouped[0], w[0, 0, :, cols], 0, 0) + dot(cot_grouped[1], w[0, 1, :, cols], 0, 0)
        part = part * g
        gh[:, at] = part
        dots[...] += v * part

    @pl.when(i == n_x - 1)
    def _():
        keys[...] = dot(pick(order[...], keys_acc.shape[0]), keys_acc[...].astype(jnp.bfloat16), 1, 0).astype(jnp.bfloat16)
        k = r * r * r * (jnp.sum(dots[...], axis=1, keepdims=True) / feats)
        for f in range(0, feats, COL):
            v = tokens[:, f : f + COL].astype(jnp.float32)
            grad[:, f : f + COL] = (r * gh[:, f : f + COL] - v * k).astype(jnp.bfloat16)


def per_device(tokens, gain, codes, scales, cotangent):
    n_y, n_x, n_z = (lax.axis_size(a) for a in ("y_hi", "x", "z"))
    rows, width = codes.shape
    toks, feats = tokens.shape
    outw = cotangent.shape[1]
    group, grouped, natural = row_orders(n_z, rows)
    half = 2 * group
    far = ("y_lo", "z", "y_hi")
    n_far = 2 * n_z * n_y

    with jax.named_scope("weight_far"):
        scale = jnp.repeat(scales.astype(jnp.float32), width // scales.shape[1], axis=1)
        own = (codes.astype(jnp.float32) * scale).astype(jnp.bfloat16)
        spread = jnp.broadcast_to(own[None], (n_far, rows, width))
        spread = lax.all_to_all(spread, far, split_axis=0, concat_axis=0, tiled=True)
        slab = spread.reshape(2, n_z, n_y, rows, width).transpose(0, 1, 3, 2, 4).reshape(2, n_z * rows, n_y * width)
        slab = jnp.pad(slab, ((0, 0), (0, group - n_z * rows), (0, 0))).reshape(half, n_y * width)
    with jax.named_scope("weight_near"):
        w = lax.all_gather(slab, ("x", "core"), axis=0, tiled=False).reshape(n_x, 2, half, n_y * width)

    gain_row = gain.reshape(1, feats)
    cot_t = cotangent.T
    with jax.named_scope("term"):
        term, cot_grouped, inv = pl.pallas_call(
            term_kernel,
            out_shape=(
                jax.ShapeDtypeStruct((2, n_x, half, n_y * width), jnp.bfloat16),
                jax.ShapeDtypeStruct((2, half, toks), jnp.bfloat16),
                jax.ShapeDtypeStruct((toks, 128), jnp.float32),
            ),
            in_specs=[VMEM] * 4,
            out_specs=(VMEM,) * 3,
            compiler_params=PARAMS,
        )(tokens, gain_row, cot_t, jnp.asarray(grouped))
    with jax.named_scope("reduce_core"):
        term, _ = lax.optimization_barrier((term, slab))
        core = lax.axis_index("core")
        mine = lax.dynamic_index_in_dim(term, core, 0, keepdims=False)
        theirs = lax.dynamic_index_in_dim(term, 1 - core, 0, keepdims=False)
        came = lax.ppermute(theirs, "core", ((0, 1), (1, 0)))
        pair = (mine.astype(jnp.float32) + came.astype(jnp.float32)).astype(jnp.bfloat16)
    with jax.named_scope("reduce_x"):
        parts = lax.all_to_all(pair, "x", split_axis=0, concat_axis=0, tiled=True)
        part = jnp.sum(parts.astype(jnp.float32), axis=0).astype(jnp.bfloat16)
    with jax.named_scope("reduce_far"):
        part = part.reshape(2, group, n_y, width)[:, : n_z * rows].reshape(2, n_z, rows, n_y, width)
        part = part.transpose(0, 1, 3, 2, 4).reshape(n_far, rows, width)
        last = lax.all_to_all(part, far, split_axis=0, concat_axis=0, tiled=True)
        grad_weight = jnp.sum(last.astype(jnp.float32), axis=0) / (n_y * n_x * n_z * 4)

    with jax.named_scope("main"):
        whole = lambda *shape: pl.BlockSpec(shape, lambda i: (0,) * len(shape))
        keys_t, grad_tokens = pl.pallas_call(
            main_kernel,
            grid=(n_x,),
            out_shape=(
                jax.ShapeDtypeStruct((outw, toks), jnp.bfloat16),
                jax.ShapeDtypeStruct((toks, feats), jnp.bfloat16),
            ),
            in_specs=[
                whole(toks, feats),
                whole(1, feats),
                whole(2, half, toks),
                whole(toks, 128),
                whole(outw, 1),
                pl.BlockSpec((1, 2, half, n_y * width), lambda i: (i, 0, 0, 0)),
            ],
            out_specs=(whole(outw, toks), whole(toks, feats)),
            scratch_shapes=[
                pltpu.VMEM((2 * half, toks), jnp.float32),
                pltpu.VMEM((toks, feats), jnp.float32),
                pltpu.VMEM((toks, COL), jnp.float32),
            ],
            compiler_params=PARAMS,
        )(tokens, gain_row, cot_grouped, inv, jnp.asarray(natural), w)
    return keys_t.T, grad_tokens, grad_weight


def solution(mesh):
    n_intra, n_inter = mesh.devices.shape
    fine = Mesh(mesh.devices.reshape(4, n_intra // 4, n_inter // 4, 2, 2), ("y_hi", "x", "z", "y_lo", "core"))
    intra, inter = ("y_hi", "x"), ("z", "y_lo", "core")
    placed = (P(intra + inter, None), P(), P(inter, intra), P(inter, intra), P(intra + inter, None))
    return jax.shard_map(
        per_device,
        mesh=fine,
        in_specs=placed,
        out_specs=(P(intra + inter, None), P(intra + inter, None), P(inter, intra)),
        check_vma=False,
    )
```

```python
import jax
import jax.numpy as jnp
from jax import lax
from jax.experimental import pallas as pl
from jax.experimental.pallas import tpu as pltpu
from jax.sharding import Mesh, PartitionSpec as P

EPS = 1e-05
COL = 256
LANE = 128
VMEM = pl.BlockSpec(memory_space=pltpu.VMEM)
SMEM = pl.BlockSpec(memory_space=pltpu.SMEM)
PARAMS = pltpu.CompilerParams(vmem_limit_bytes=48 * 1024 * 1024)


def dot(a, b, ca, cb):
    return lax.dot_general(a, b, (((ca,), (cb,)), ((), ())), preferred_element_type=jnp.float32)


def term_kernel(n_y, n_x, place, tokens, gain, cot, mine, theirs, inv):
    feats = tokens.shape[1]
    total = jnp.zeros((tokens.shape[0], COL), jnp.float32)
    for f in range(0, feats, COL):
        v = tokens[:, f : f + COL].astype(jnp.float32)
        total = total + v * v
    r = lax.rsqrt(jnp.sum(total, axis=1, keepdims=True) / feats + EPS)
    inv[...] = jnp.broadcast_to(r, inv.shape)
    second = place[2] == 1
    for f in range(0, feats, COL):
        v = tokens[:, f : f + COL].astype(jnp.float32)
        hid = (v * r * gain[:, f : f + COL].astype(jnp.float32)).astype(jnp.bfloat16)
        y, x = divmod(f // COL, n_x)
        part = dot(cot[...], hid, 1, 0).astype(jnp.bfloat16)
        low, high = part[:, :LANE], part[:, LANE:]
        a, b = lax.rem(x + n_x - place[1], n_x), lax.rem(y + n_y - place[0], n_y)
        mine[a, b] = jnp.where(second, high, low)
        theirs[a, b] = jnp.where(second, low, high)


def main_kernel(n_y, place, tokens, gain, cot, inv, w, keys, grad, keys_acc, gh, dots):
    i = pl.program_id(0)
    n_x = pl.num_programs(0)
    toks, feats = tokens.shape
    r = inv[:, :1]

    @pl.when(i == 0)
    def _():
        keys_acc[...] = jnp.zeros_like(keys_acc)
        dots[...] = jnp.zeros_like(dots)

    for s in range(n_y):
        y = lax.rem(place[0] + n_y - s, n_y)
        at = pl.ds(pl.multiple_of((y * n_x + i) * COL, COL), COL)
        v = tokens[:, at].astype(jnp.float32)
        g = gain[:, at].astype(jnp.float32)
        hid = (v * r * g).astype(jnp.bfloat16)
        weight = jnp.concatenate([w[0, 0, s], w[0, 1, s]], axis=1)
        keys_acc[...] += dot(weight, hid, 1, 1)
        part = dot(cot[...], weight, 0, 0) * g
        gh[:, at] = part
        dots[...] += v * part

    @pl.when(i == n_x - 1)
    def _():
        keys[...] = keys_acc[...].astype(jnp.bfloat16)
        k = r * r * r * (jnp.sum(dots[...], axis=1, keepdims=True) / feats)
        for f in range(0, feats, COL):
            v = tokens[:, f : f + COL].astype(jnp.float32)
            grad[:, f : f + COL] = (r * gh[:, f : f + COL] - v * k).astype(jnp.bfloat16)


def shifted(value, axis, s):
    n = lax.axis_size(axis)
    return lax.ppermute(value, axis, [(j, (j + s) % n) for j in range(n)])


def add(values):
    total = values[0].astype(jnp.float32)
    for value in values[1:]:
        total = total + value.astype(jnp.float32)
    return total


def per_device(tokens, gain, codes, scales, cotangent):
    n_y, n_x, n_z = (lax.axis_size(a) for a in ("y_hi", "x", "z"))
    rows, width = codes.shape
    toks, feats = tokens.shape
    outw = cotangent.shape[1]
    inter = ("z", "y_lo", "core")
    n_inter = 4 * n_z
    place = jnp.stack([lax.axis_index(a) for a in ("y_hi", "x", "core")]).astype(jnp.int32)
    gain_row = gain.reshape(1, feats)
    cot_t = cotangent.T

    with jax.named_scope("term"):
        near = jax.ShapeDtypeStruct((n_x, n_y, outw, LANE), jnp.bfloat16)
        mine, theirs, inv = pl.pallas_call(
            lambda *refs: term_kernel(n_y, n_x, *refs),
            out_shape=(near, near, jax.ShapeDtypeStruct((toks, LANE), jnp.float32)),
            in_specs=[SMEM] + [VMEM] * 3,
            out_specs=(VMEM,) * 3,
            compiler_params=PARAMS,
        )(place, tokens, gain_row, cot_t)
    with jax.named_scope("reduce_core"):
        came = lax.ppermute(theirs, "core", ((0, 1), (1, 0)))

    with jax.named_scope("weight_far"):
        scale = jnp.repeat(scales.astype(jnp.float32), width // scales.shape[1], axis=1)
        own = (codes.astype(jnp.float32) * scale).astype(jnp.bfloat16)
        own, _ = lax.optimization_barrier((own, theirs))
        halves = jnp.stack([own[:, :LANE], own[:, LANE:]])
        spread = jnp.broadcast_to(halves[None], (n_inter // 2, 2, rows, LANE)).reshape(n_inter, rows, LANE)
        spread = lax.all_to_all(spread, inter, split_axis=0, concat_axis=0, tiled=True)
        strip = spread.reshape(outw, LANE)
    with jax.named_scope("weight_y"):
        slab = jnp.stack([strip] + [shifted(strip, "y_hi", s) for s in range(1, n_y)])
    with jax.named_scope("weight_near"):
        w = lax.all_gather(slab, ("x", "core"), axis=0, tiled=False).reshape(n_x, 2, n_y, outw, LANE)

    with jax.named_scope("reduce_x"):
        pairs = [add([mine[s], came[s]]).astype(jnp.bfloat16) for s in range(n_x)]
        part = add([pairs[0]] + [shifted(pairs[s], "x", s) for s in range(1, n_x)]).astype(jnp.bfloat16)
    with jax.named_scope("reduce_y"):
        part = add([part[0]] + [shifted(part[s], "y_hi", s) for s in range(1, n_y)]).astype(jnp.bfloat16)
    with jax.named_scope("reduce_far"):
        last = lax.all_to_all(part.reshape(n_inter, rows, LANE), inter, split_axis=0, concat_axis=0, tiled=True)
        last = jnp.sum(last.reshape(n_inter // 2, 2, rows, LANE).astype(jnp.float32), axis=0)
        grad_weight = jnp.concatenate([last[0], last[1]], axis=1) / (n_y * n_x * n_inter)

    with jax.named_scope("main"):
        whole = lambda *shape: pl.BlockSpec(shape, lambda i: (0,) * len(shape))
        keys_t, grad_tokens = pl.pallas_call(
            lambda *refs: main_kernel(n_y, *refs),
            grid=(n_x,),
            out_shape=(
                jax.ShapeDtypeStruct((outw, toks), jnp.bfloat16),
                jax.ShapeDtypeStruct((toks, feats), jnp.bfloat16),
            ),
            in_specs=[
                SMEM,
                whole(toks, feats),
                whole(1, feats),
                whole(outw, toks),
                whole(toks, LANE),
                pl.BlockSpec((1, 2, n_y, outw, LANE), lambda i: (i, 0, 0, 0, 0)),
            ],
            out_specs=(whole(outw, toks), whole(toks, feats)),
            scratch_shapes=[
                pltpu.VMEM((outw, toks), jnp.float32),
                pltpu.VMEM((toks, feats), jnp.float32),
                pltpu.VMEM((toks, COL), jnp.float32),
            ],
            compiler_params=PARAMS,
        )(place, tokens, gain_row, cot_t, inv, w)
    return keys_t.T, grad_tokens, grad_weight


def solution(mesh):
    n_intra, n_inter = mesh.devices.shape
    fine = Mesh(mesh.devices.reshape(4, n_intra // 4, n_inter // 4, 2, 2), ("y_hi", "x", "z", "y_lo", "core"))
    intra, inter = ("y_hi", "x"), ("z", "y_lo", "core")
    placed = (P(intra + inter, None), P(), P(inter, intra), P(inter, intra), P(intra + inter, None))
    return jax.shard_map(
        per_device,
        mesh=fine,
        in_specs=placed,
        out_specs=(P(intra + inter, None), P(intra + inter, None), P(inter, intra)),
        check_vma=False,
    )
```

```python
import numpy as np
import jax
import jax.numpy as jnp
from jax import lax
from jax.experimental import pallas as pl
from jax.experimental.pallas import tpu as pltpu
from jax.sharding import Mesh, PartitionSpec as P

EPS = 1e-05
COL = 256
LANE = 128
VMEM = pl.BlockSpec(memory_space=pltpu.VMEM)
SMEM = pl.BlockSpec(memory_space=pltpu.SMEM)
PARAMS = pltpu.CompilerParams(vmem_limit_bytes=48 * 1024 * 1024)


def row_orders(n_z, rows):
    group = -(-n_z * rows // 8) * 8
    grouped = np.full((4 * group, 1), -1, np.int32)
    natural = np.zeros((n_z * 4 * rows, 1), np.int32)
    for z in range(n_z):
        for y in range(2):
            for c in range(2):
                for r in range(rows):
                    o = ((z * 2 + y) * 2 + c) * rows + r
                    p = (c * 2 + y) * group + z * rows + r
                    grouped[p, 0] = o
                    natural[o, 0] = p
    return group, grouped, natural


def pick(index, width):
    lanes = lax.broadcasted_iota(jnp.int32, (index.shape[0], width), 1)
    return jnp.where(lanes == index, 1.0, 0.0).astype(jnp.bfloat16)


def dot(a, b, ca, cb):
    return lax.dot_general(a, b, (((ca,), (cb,)), ((), ())), preferred_element_type=jnp.float32)


def term_kernel(n_x, place, tokens, gain, cot, order, mine, theirs, cot_grouped, inv):
    feats = tokens.shape[1]
    half, group = order.shape[0] // 2, order.shape[0] // 4
    total = jnp.zeros((tokens.shape[0], COL), jnp.float32)
    for f in range(0, feats, COL):
        v = tokens[:, f : f + COL].astype(jnp.float32)
        total = total + v * v
    r = lax.rsqrt(jnp.sum(total, axis=1, keepdims=True) / feats + EPS)
    inv[...] = jnp.broadcast_to(r, inv.shape)
    for c in range(2):
        chosen = pick(order[c * half : (c + 1) * half, :], cot.shape[0])
        cot_grouped[c] = dot(chosen, cot[...], 1, 0).astype(jnp.bfloat16)
    for f in range(0, feats, COL):
        v = tokens[:, f : f + COL].astype(jnp.float32)
        hid = (v * r * gain[:, f : f + COL].astype(jnp.float32)).astype(jnp.bfloat16)
        y, x = divmod(f // COL, n_x)
        for out, c in ((theirs, 1 - place[0]), (mine, place[0])):
            part = dot(cot_grouped[c], hid, 1, 0)
            out[x, 2 * y] = part[:group].astype(jnp.bfloat16)
            out[x, 2 * y + 1] = part[group:].astype(jnp.bfloat16)


def main_kernel(tokens, gain, cot_grouped, inv, order, w, keys, grad, keys_acc, gh, dots):
    i = pl.program_id(0)
    toks, feats = tokens.shape
    n_x = w.shape[3]
    r = inv[:, :1]

    @pl.when(i == 0)
    def _():
        keys_acc[...] = jnp.zeros_like(keys_acc)
        dots[...] = jnp.zeros_like(dots)

    for x in range(n_x):
        at = pl.ds(pl.multiple_of((i * n_x + x) * COL, COL), COL)
        v = tokens[:, at].astype(jnp.float32)
        g = gain[:, at].astype(jnp.float32)
        hid = (v * r * g).astype(jnp.bfloat16)
        weight = jnp.concatenate([w[0, y, c, x] for c in range(2) for y in range(2)], axis=0)
        keys_acc[...] += dot(weight, hid, 1, 1)
        part = dot(cot_grouped[...], weight, 0, 0) * g
        gh[:, at] = part
        dots[...] += v * part

    @pl.when(i == pl.num_programs(0) - 1)
    def _():
        keys[...] = dot(pick(order[...], keys_acc.shape[0]), keys_acc[...].astype(jnp.bfloat16), 1, 0).astype(jnp.bfloat16)
        k = r * r * r * (jnp.sum(dots[...], axis=1, keepdims=True) / feats)
        for f in range(0, feats, COL):
            v = tokens[:, f : f + COL].astype(jnp.float32)
            grad[:, f : f + COL] = (r * gh[:, f : f + COL] - v * k).astype(jnp.bfloat16)


def per_device(tokens, gain, codes, scales, cotangent):
    n_y, n_x, n_z = (lax.axis_size(a) for a in ("y_hi", "x", "z"))
    rows, width = codes.shape
    toks, feats = tokens.shape
    outw = cotangent.shape[1]
    group, grouped, natural = row_orders(n_z, rows)
    place = lax.axis_index("core").astype(jnp.int32).reshape(1)
    gain_row = gain.reshape(1, feats)
    cot_t = cotangent.T

    with jax.named_scope("weight_far"):
        scale = jnp.repeat(scales.astype(jnp.float32), width // scales.shape[1], axis=1)
        own = (codes.astype(jnp.float32) * scale).astype(jnp.bfloat16)
        spread = jnp.broadcast_to(own[None], (n_x * n_z, rows, width))
        spread = lax.all_to_all(spread, ("x", "z"), split_axis=0, concat_axis=0, tiled=True)
        slab = jnp.pad(spread.reshape(n_x, n_z * rows, width), ((0, 0), (0, group - n_z * rows), (0, 0)))
    with jax.named_scope("weight_near"):
        w = lax.all_gather(slab, ("y_hi", "y_lo", "core"), axis=0, tiled=False).reshape(n_y, 2, 2, n_x, group, width)

    with jax.named_scope("term"):
        near = jax.ShapeDtypeStruct((n_x, 2 * n_y, group, width), jnp.bfloat16)
        mine, theirs, cot_grouped, inv = pl.pallas_call(
            lambda *refs: term_kernel(n_x, *refs),
            out_shape=(
                near,
                near,
                jax.ShapeDtypeStruct((2, 2 * group, toks), jnp.bfloat16),
                jax.ShapeDtypeStruct((toks, LANE), jnp.float32),
            ),
            in_specs=[SMEM] + [VMEM] * 4,
            out_specs=(VMEM,) * 4,
            compiler_params=PARAMS,
            cost_estimate=pl.CostEstimate(flops=3 * toks * outw * feats, bytes_accessed=4 * toks * feats, transcendentals=0),
        )(place, tokens, gain_row, cot_t, jnp.asarray(grouped))
        cot_grouped = cot_grouped.reshape(4 * group, toks)
    with jax.named_scope("reduce_core"):
        came = lax.ppermute(theirs, "core", ((0, 1), (1, 0)))
        came, _ = lax.optimization_barrier((came, slab))
        pair = (mine.astype(jnp.float32) + came.astype(jnp.float32)).astype(jnp.bfloat16)
    with jax.named_scope("reduce_x"):
        parts = lax.all_to_all(pair, "x", split_axis=0, concat_axis=0, tiled=True)
        part = jnp.sum(parts.astype(jnp.float32), axis=0).astype(jnp.bfloat16)
    with jax.named_scope("reduce_y"):
        parts = lax.all_to_all(part, ("y_hi", "y_lo"), split_axis=0, concat_axis=0, tiled=True)
        part = jnp.sum(parts.astype(jnp.float32), axis=0).astype(jnp.bfloat16)
    with jax.named_scope("reduce_z"):
        last = lax.all_to_all(part[: n_z * rows].reshape(n_z, rows, width), "z", split_axis=0, concat_axis=0, tiled=True)
        grad_weight = jnp.sum(last.astype(jnp.float32), axis=0) / (n_y * n_x * n_z * 4)

    with jax.named_scope("main"):
        whole = lambda *shape: pl.BlockSpec(shape, lambda i: (0,) * len(shape))
        keys_t, grad_tokens = pl.pallas_call(
            main_kernel,
            grid=(n_y,),
            out_shape=(
                jax.ShapeDtypeStruct((outw, toks), jnp.bfloat16),
                jax.ShapeDtypeStruct((toks, feats), jnp.bfloat16),
            ),
            in_specs=[
                whole(toks, feats),
                whole(1, feats),
                whole(4 * group, toks),
                whole(toks, LANE),
                whole(outw, 1),
                pl.BlockSpec((1, 2, 2, n_x, group, width), lambda i: (i, 0, 0, 0, 0, 0)),
            ],
            out_specs=(whole(outw, toks), whole(toks, feats)),
            scratch_shapes=[
                pltpu.VMEM((4 * group, toks), jnp.float32),
                pltpu.VMEM((toks, feats), jnp.float32),
                pltpu.VMEM((toks, COL), jnp.float32),
            ],
            compiler_params=PARAMS,
            cost_estimate=pl.CostEstimate(flops=5 * toks * outw * feats, bytes_accessed=10 * toks * feats, transcendentals=0),
        )(tokens, gain_row, cot_grouped, inv, jnp.asarray(natural), w)
    return keys_t.T, grad_tokens, grad_weight


def solution(mesh):
    n_intra, n_inter = mesh.devices.shape
    fine = Mesh(mesh.devices.reshape(4, n_intra // 4, n_inter // 4, 2, 2), ("y_hi", "x", "z", "y_lo", "core"))
    intra, inter = ("y_hi", "x"), ("z", "y_lo", "core")
    placed = (P(intra + inter, None), P(), P(inter, intra), P(inter, intra), P(intra + inter, None))
    return jax.shard_map(
        per_device,
        mesh=fine,
        in_specs=placed,
        out_specs=(P(intra + inter, None), P(intra + inter, None), P(inter, intra)),
        check_vma=False,
    )
```

```python
import numpy as np
import jax
import jax.numpy as jnp
from jax import lax
from jax.experimental import pallas as pl
from jax.experimental.pallas import tpu as pltpu
from jax.sharding import Mesh, PartitionSpec as P

EPS = 1e-05
COL = 256
LANE = 128
VMEM = pl.BlockSpec(memory_space=pltpu.VMEM)
SMEM = pl.BlockSpec(memory_space=pltpu.SMEM)
PARAMS = pltpu.CompilerParams(vmem_limit_bytes=48 * 1024 * 1024)


def row_orders(n_z, rows):
    group = -(-n_z * rows // 8) * 8
    grouped = np.full((4 * group, 1), -1, np.int32)
    natural = np.zeros((n_z * 4 * rows, 1), np.int32)
    for z in range(n_z):
        for y in range(2):
            for c in range(2):
                for r in range(rows):
                    o = ((z * 2 + y) * 2 + c) * rows + r
                    p = (c * 2 + y) * group + z * rows + r
                    grouped[p, 0] = o
                    natural[o, 0] = p
    return group, grouped, natural


def pick(index, width):
    lanes = lax.broadcasted_iota(jnp.int32, (index.shape[0], width), 1)
    return jnp.where(lanes == index, 1.0, 0.0).astype(jnp.bfloat16)


def dot(a, b, ca, cb):
    return lax.dot_general(a, b, (((ca,), (cb,)), ((), ())), preferred_element_type=jnp.float32)


def term_kernel(n_x, place, tokens, gain, cot, order, mine, theirs, cot_grouped, inv):
    feats = tokens.shape[1]
    half, group = order.shape[0] // 2, order.shape[0] // 4
    total = jnp.zeros((tokens.shape[0], COL), jnp.float32)
    for f in range(0, feats, COL):
        v = tokens[:, f : f + COL].astype(jnp.float32)
        total = total + v * v
    r = lax.rsqrt(jnp.sum(total, axis=1, keepdims=True) / feats + EPS)
    inv[...] = jnp.broadcast_to(r, inv.shape)
    for c in range(2):
        chosen = pick(order[c * half : (c + 1) * half, :], cot.shape[0])
        cot_grouped[c] = dot(chosen, cot[...], 1, 0).astype(jnp.bfloat16)
    for f in range(0, feats, COL):
        v = tokens[:, f : f + COL].astype(jnp.float32)
        hid = (v * r * gain[:, f : f + COL].astype(jnp.float32)).astype(jnp.bfloat16)
        y, x = divmod(f // COL, n_x)
        for out, c in ((theirs, 1 - place[0]), (mine, place[0])):
            part = dot(cot_grouped[c], hid, 1, 0)
            out[x, 2 * y] = part[:group].astype(jnp.bfloat16)
            out[x, 2 * y + 1] = part[group:].astype(jnp.bfloat16)


def prep_kernel(tokens, gain, cot_grouped, inv, hid, cot):
    r = inv[:, :1]
    for f in range(0, tokens.shape[1], COL):
        v = tokens[:, f : f + COL].astype(jnp.float32)
        hid[:, f : f + COL] = (v * r * gain[:, f : f + COL].astype(jnp.float32)).astype(jnp.bfloat16)
    cot[...] = cot_grouped[...].T


def main_kernel(tokens, gain, hid, cot, inv, back, w, keys, grad, keys_acc, gh, dots):
    i = pl.program_id(0)
    toks, feats = tokens.shape
    n_x = w.shape[3]
    r = inv[:, :1]

    @pl.when(i == 0)
    def _():
        keys_acc[...] = jnp.zeros_like(keys_acc)
        dots[...] = jnp.zeros_like(dots)

    for x in range(n_x):
        at = pl.ds(pl.multiple_of((i * n_x + x) * COL, COL), COL)
        v = tokens[:, at].astype(jnp.float32)
        weight = jnp.concatenate([w[0, y, c, x] for c in range(2) for y in range(2)], axis=0)
        keys_acc[...] += dot(weight, hid[:, at], 1, 1)
        part = dot(cot[...], weight, 1, 0) * gain[:, at].astype(jnp.float32)
        gh[:, at] = part
        dots[...] += v * part

    @pl.when(i == pl.num_programs(0) - 1)
    def _():
        keys[...] = dot(back[...], keys_acc[...].astype(jnp.bfloat16), 1, 0).astype(jnp.bfloat16)
        k = r * r * r * (jnp.sum(dots[...], axis=1, keepdims=True) / feats)
        for f in range(0, feats, COL):
            v = tokens[:, f : f + COL].astype(jnp.float32)
            grad[:, f : f + COL] = (r * gh[:, f : f + COL] - v * k).astype(jnp.bfloat16)


def add(values):
    total = values[0].astype(jnp.float32)
    for i in range(1, values.shape[0]):
        total = total + values[i].astype(jnp.float32)
    return total


def together(*values):
    return lax.optimization_barrier(values)


def per_device(tokens, gain, codes, scales, cotangent):
    n_y, n_x, n_z = (lax.axis_size(a) for a in ("y_hi", "x", "z"))
    rows, width = codes.shape
    toks, feats = tokens.shape
    outw = cotangent.shape[1]
    group, grouped, natural = row_orders(n_z, rows)
    place = lax.axis_index("core").astype(jnp.int32).reshape(1)
    gain_row = gain.reshape(1, feats)
    cot_t = cotangent.T

    with jax.named_scope("weight_far"):
        scale = jnp.repeat(scales.astype(jnp.float32), width // scales.shape[1], axis=1)
        own = (codes.astype(jnp.float32) * scale).astype(jnp.bfloat16)
        spread = jnp.broadcast_to(own[None], (n_x * n_z, rows, width))
        spread, tokens_after = together(spread, tokens)
        spread = lax.all_to_all(spread, ("x", "z"), split_axis=0, concat_axis=0, tiled=True)
    with jax.named_scope("term"):
        near = jax.ShapeDtypeStruct((n_x, 2 * n_y, group, width), jnp.bfloat16)
        mine, theirs, cot_grouped, inv = pl.pallas_call(
            lambda *refs: term_kernel(n_x, *refs),
            out_shape=(
                near,
                near,
                jax.ShapeDtypeStruct((2, 2 * group, toks), jnp.bfloat16),
                jax.ShapeDtypeStruct((toks, LANE), jnp.float32),
            ),
            in_specs=[SMEM] + [VMEM] * 4,
            out_specs=(VMEM,) * 4,
            compiler_params=PARAMS,
            cost_estimate=pl.CostEstimate(flops=3 * toks * outw * feats, bytes_accessed=4 * toks * feats, transcendentals=0),
        )(place, tokens_after, gain_row, cot_t, jnp.asarray(grouped))
        cot_grouped = cot_grouped.reshape(4 * group, toks)
    with jax.named_scope("weight_near"):
        came = lax.ppermute(theirs, "core", ((0, 1), (1, 0)))
        spread, came = together(spread, came)
        slab = jnp.pad(spread.reshape(n_x, n_z * rows, width), ((0, 0), (0, group - n_z * rows), (0, 0)))
        w = lax.all_gather(slab, ("y_hi", "y_lo", "core"), axis=0, tiled=False).reshape(n_y, 2, 2, n_x, group, width)
    with jax.named_scope("reduce_core"):
        came, _ = together(came, slab)
        pair = (mine.astype(jnp.float32) + came.astype(jnp.float32)).astype(jnp.bfloat16)
    with jax.named_scope("reduce_x"):
        pair, inv = together(pair, inv)
        parts = lax.all_to_all(pair, "x", split_axis=0, concat_axis=0, tiled=True)
        hid, cot = pl.pallas_call(
            prep_kernel,
            out_shape=(
                jax.ShapeDtypeStruct((toks, feats), jnp.bfloat16),
                jax.ShapeDtypeStruct((toks, 4 * group), jnp.bfloat16),
            ),
            in_specs=[VMEM] * 4,
            out_specs=(VMEM,) * 2,
            compiler_params=PARAMS,
            cost_estimate=pl.CostEstimate(flops=4 * toks * feats, bytes_accessed=4 * toks * feats, transcendentals=0),
        )(tokens, gain_row, cot_grouped, inv)
        parts, hid = together(parts, hid)
        part = add(parts).astype(jnp.bfloat16)
    with jax.named_scope("reduce_y"):
        part, order = together(part, jnp.asarray(natural))
        parts = lax.all_to_all(part, ("y_hi", "y_lo"), split_axis=0, concat_axis=0, tiled=True)
        back = pick(order, 4 * group)
        parts, back = together(parts, back)
        part = add(parts).astype(jnp.bfloat16)[: n_z * rows].reshape(n_z, rows, width)
    with jax.named_scope("reduce_z"):
        part, back = together(part, back)
        last = lax.all_to_all(part, "z", split_axis=0, concat_axis=0, tiled=True)
    with jax.named_scope("main"):
        whole = lambda *shape: pl.BlockSpec(shape, lambda i: (0,) * len(shape))
        keys_t, grad_tokens = pl.pallas_call(
            main_kernel,
            grid=(n_y,),
            out_shape=(
                jax.ShapeDtypeStruct((outw, toks), jnp.bfloat16),
                jax.ShapeDtypeStruct((toks, feats), jnp.bfloat16),
            ),
            in_specs=[
                whole(toks, feats),
                whole(1, feats),
                whole(toks, feats),
                whole(toks, 4 * group),
                whole(toks, LANE),
                whole(outw, 4 * group),
                pl.BlockSpec((1, 2, 2, n_x, group, width), lambda i: (i, 0, 0, 0, 0, 0)),
            ],
            out_specs=(whole(outw, toks), whole(toks, feats)),
            scratch_shapes=[
                pltpu.VMEM((4 * group, toks), jnp.float32),
                pltpu.VMEM((toks, feats), jnp.float32),
                pltpu.VMEM((toks, COL), jnp.float32),
            ],
            compiler_params=PARAMS,
            cost_estimate=pl.CostEstimate(flops=5 * toks * outw * feats, bytes_accessed=10 * toks * feats, transcendentals=0),
        )(tokens, gain_row, hid, cot, inv, back, w)
    with jax.named_scope("finish"):
        last, keys_t = together(last, keys_t)
        grad_weight = jnp.sum(last.astype(jnp.float32), axis=0) / (n_y * n_x * n_z * 4)
    return keys_t.T, grad_tokens, grad_weight


def solution(mesh):
    n_intra, n_inter = mesh.devices.shape
    fine = Mesh(mesh.devices.reshape(4, n_intra // 4, n_inter // 4, 2, 2), ("y_hi", "x", "z", "y_lo", "core"))
    intra, inter = ("y_hi", "x"), ("z", "y_lo", "core")
    placed = (P(intra + inter, None), P(), P(inter, intra), P(inter, intra), P(intra + inter, None))
    return jax.shard_map(
        per_device,
        mesh=fine,
        in_specs=placed,
        out_specs=(P(intra + inter, None), P(intra + inter, None), P(inter, intra)),
        check_vma=False,
    )
```

```python
import numpy as np
import jax
import jax.numpy as jnp
from jax import lax
from jax.experimental import pallas as pl
from jax.experimental.pallas import tpu as pltpu
from jax.sharding import Mesh, PartitionSpec as P

EPS = 1e-05
COL = 256
LANE = 128
VMEM = pl.BlockSpec(memory_space=pltpu.VMEM)
SMEM = pl.BlockSpec(memory_space=pltpu.SMEM)


def params(mib):
    return pltpu.CompilerParams(vmem_limit_bytes=mib * 1024 * 1024)


def row_orders(n_z, rows):
    group = -(-n_z * rows // 8) * 8
    grouped = np.full((4 * group, 1), -1, np.int32)
    natural = np.zeros((n_z * 4 * rows, 1), np.int32)
    for z in range(n_z):
        for y in range(2):
            for c in range(2):
                for r in range(rows):
                    o = ((z * 2 + y) * 2 + c) * rows + r
                    p = (c * 2 + y) * group + z * rows + r
                    grouped[p, 0] = o
                    natural[o, 0] = p
    return group, grouped, natural


def pick(index, width):
    lanes = lax.broadcasted_iota(jnp.int32, (index.shape[0], width), 1)
    return jnp.where(lanes == index, 1.0, 0.0).astype(jnp.bfloat16)


def dot(a, b, ca, cb):
    return lax.dot_general(a, b, (((ca,), (cb,)), ((), ())), preferred_element_type=jnp.float32)


def term_kernel(n_x, place, tokens, gain, cot, order, mine, theirs, cot_grouped, inv):
    feats = tokens.shape[1]
    half, group = order.shape[0] // 2, order.shape[0] // 4
    total = jnp.zeros((tokens.shape[0], COL), jnp.float32)
    for f in range(0, feats, COL):
        v = tokens[:, f : f + COL].astype(jnp.float32)
        total = total + v * v
    r = lax.rsqrt(jnp.sum(total, axis=1, keepdims=True) / feats + EPS)
    inv[...] = jnp.broadcast_to(r, inv.shape)
    for c in range(2):
        chosen = pick(order[c * half : (c + 1) * half, :], cot.shape[0])
        cot_grouped[c] = dot(chosen, cot[...], 1, 0).astype(jnp.bfloat16)
    for f in range(0, feats, COL):
        v = tokens[:, f : f + COL].astype(jnp.float32)
        hid = (v * r * gain[:, f : f + COL].astype(jnp.float32)).astype(jnp.bfloat16)
        y, x = divmod(f // COL, n_x)
        for out, c in ((theirs, 1 - place[0]), (mine, place[0])):
            part = dot(cot_grouped[c], hid, 1, 0)
            out[x, 2 * y] = part[:group].astype(jnp.bfloat16)
            out[x, 2 * y + 1] = part[group:].astype(jnp.bfloat16)


def prep_kernel(cot_grouped, cot):
    cot[...] = cot_grouped[...].T


def main_kernel(tokens, gain, cot, inv, back, w, keys, grad, keys_acc, gh, dots):
    i = pl.program_id(0)
    toks, feats = tokens.shape
    n_x = w.shape[3]
    r = inv[:, :1]

    @pl.when(i == 0)
    def _():
        keys_acc[...] = jnp.zeros_like(keys_acc)
        dots[...] = jnp.zeros_like(dots)

    for x in range(n_x):
        at = pl.ds(pl.multiple_of((i * n_x + x) * COL, COL), COL)
        v = tokens[:, at].astype(jnp.float32)
        g = gain[:, at].astype(jnp.float32)
        hid = (v * r * g).astype(jnp.bfloat16)
        weight = jnp.concatenate([w[0, y, c, x] for c in range(2) for y in range(2)], axis=0)
        keys_acc[...] += dot(weight, hid, 1, 1)
        part = dot(cot[...], weight, 1, 0) * g
        gh[:, at] = part
        dots[...] += v * part

    @pl.when(i == pl.num_programs(0) - 1)
    def _():
        keys[...] = dot(back[...], keys_acc[...].astype(jnp.bfloat16), 1, 0).astype(jnp.bfloat16)
        k = r * r * r * (jnp.sum(dots[...], axis=1, keepdims=True) / feats)
        for f in range(0, feats, COL):
            v = tokens[:, f : f + COL].astype(jnp.float32)
            grad[:, f : f + COL] = (r * gh[:, f : f + COL] - v * k).astype(jnp.bfloat16)


def add(values):
    total = values[0].astype(jnp.float32)
    for i in range(1, values.shape[0]):
        total = total + values[i].astype(jnp.float32)
    return total


def together(*values):
    return lax.optimization_barrier(values)


def per_device(tokens, gain, codes, scales, cotangent):
    n_y, n_x, n_z = (lax.axis_size(a) for a in ("y_hi", "x", "z"))
    rows, width = codes.shape
    toks, feats = tokens.shape
    outw = cotangent.shape[1]
    group, grouped, natural = row_orders(n_z, rows)
    place = lax.axis_index("core").astype(jnp.int32).reshape(1)
    gain_row = gain.reshape(1, feats)
    cot_t = cotangent.T

    with jax.named_scope("weight_far"):
        scale = jnp.repeat(scales.astype(jnp.float32), width // scales.shape[1], axis=1)
        own = (codes.astype(jnp.float32) * scale).astype(jnp.bfloat16)
        spread = jnp.broadcast_to(own[None], (n_x * n_z, rows, width))
        spread, tokens_after = together(spread, tokens)
        spread = lax.all_to_all(spread, ("x", "z"), split_axis=0, concat_axis=0, tiled=True)
    with jax.named_scope("term"):
        near = jax.ShapeDtypeStruct((n_x, 2 * n_y, group, width), jnp.bfloat16)
        mine, theirs, cot_grouped, inv = pl.pallas_call(
            lambda *refs: term_kernel(n_x, *refs),
            out_shape=(
                near,
                near,
                jax.ShapeDtypeStruct((2, 2 * group, toks), jnp.bfloat16),
                jax.ShapeDtypeStruct((toks, LANE), jnp.float32),
            ),
            in_specs=[SMEM] + [VMEM] * 4,
            out_specs=(VMEM,) * 4,
            compiler_params=params(20),
            cost_estimate=pl.CostEstimate(flops=3 * toks * outw * feats, bytes_accessed=4 * toks * feats, transcendentals=0),
        )(place, tokens_after, gain_row, cot_t, jnp.asarray(grouped))
        cot_grouped = cot_grouped.reshape(4 * group, toks)
    with jax.named_scope("weight_near"):
        spread, theirs = together(spread, theirs)
        slab = jnp.pad(spread.reshape(n_x, n_z * rows, width), ((0, 0), (0, group - n_z * rows), (0, 0)))
        w = lax.all_gather(slab, ("y_hi", "y_lo", "core"), axis=0, tiled=False).reshape(n_y, 2, 2, n_x, group, width)
    with jax.named_scope("reduce_core"):
        theirs, _ = together(theirs, slab)
        came = lax.ppermute(theirs, "core", ((0, 1), (1, 0)))
        pair = (mine.astype(jnp.float32) + came.astype(jnp.float32)).astype(jnp.bfloat16)
    with jax.named_scope("reduce_x"):
        pair, cot_after, _ = together(pair, cot_grouped, slab)
        parts = lax.all_to_all(pair, "x", split_axis=0, concat_axis=0, tiled=True)
        cot = pl.pallas_call(
            prep_kernel,
            out_shape=jax.ShapeDtypeStruct((toks, 4 * group), jnp.bfloat16),
            in_specs=[VMEM],
            out_specs=VMEM,
            compiler_params=params(8),
        )(cot_after)
        parts, cot = together(parts, cot)
        part = add(parts).astype(jnp.bfloat16)
    with jax.named_scope("reduce_y"):
        part, order = together(part, jnp.asarray(natural))
        parts = lax.all_to_all(part, ("y_hi", "y_lo"), split_axis=0, concat_axis=0, tiled=True)
        back = pick(order, 4 * group)
        parts, back = together(parts, back)
        part = add(parts).astype(jnp.bfloat16)[: n_z * rows].reshape(n_z, rows, width)
    with jax.named_scope("reduce_z"):
        part, back = together(part, back)
        last = lax.all_to_all(part, "z", split_axis=0, concat_axis=0, tiled=True)
    with jax.named_scope("main"):
        whole = lambda *shape: pl.BlockSpec(shape, lambda i: (0,) * len(shape))
        keys_t, grad_tokens = pl.pallas_call(
            main_kernel,
            grid=(n_y,),
            out_shape=(
                jax.ShapeDtypeStruct((outw, toks), jnp.bfloat16),
                jax.ShapeDtypeStruct((toks, feats), jnp.bfloat16),
            ),
            in_specs=[
                whole(toks, feats),
                whole(1, feats),
                whole(toks, 4 * group),
                whole(toks, LANE),
                whole(outw, 4 * group),
                pl.BlockSpec((1, 2, 2, n_x, group, width), lambda i: (i, 0, 0, 0, 0, 0)),
            ],
            out_specs=(whole(outw, toks), whole(toks, feats)),
            scratch_shapes=[
                pltpu.VMEM((4 * group, toks), jnp.float32),
                pltpu.VMEM((toks, feats), jnp.float32),
                pltpu.VMEM((toks, COL), jnp.float32),
            ],
            compiler_params=params(60),
            cost_estimate=pl.CostEstimate(flops=5 * toks * outw * feats, bytes_accessed=10 * toks * feats, transcendentals=0),
        )(tokens, gain_row, cot, inv, back, w)
    with jax.named_scope("finish"):
        last, keys_t = together(last, keys_t)
        grad_weight = jnp.sum(last.astype(jnp.float32), axis=0) / (n_y * n_x * n_z * 4)
    return keys_t.T, grad_tokens, grad_weight


def solution(mesh):
    n_intra, n_inter = mesh.devices.shape
    fine = Mesh(mesh.devices.reshape(4, n_intra // 4, n_inter // 4, 2, 2), ("y_hi", "x", "z", "y_lo", "core"))
    intra, inter = ("y_hi", "x"), ("z", "y_lo", "core")
    placed = (P(intra + inter, None), P(), P(inter, intra), P(inter, intra), P(intra + inter, None))
    return jax.shard_map(
        per_device,
        mesh=fine,
        in_specs=placed,
        out_specs=(P(intra + inter, None), P(intra + inter, None), P(inter, intra)),
        check_vma=False,
    )
```

```python
import numpy as np
import jax
import jax.numpy as jnp
from jax import lax
from jax.experimental import pallas as pl
from jax.experimental.pallas import tpu as pltpu
from jax.sharding import Mesh, PartitionSpec as P

EPS = 1e-05
COL = 256
LANE = 128
VMEM = pl.BlockSpec(memory_space=pltpu.VMEM)
SMEM = pl.BlockSpec(memory_space=pltpu.SMEM)


def params(mib):
    return pltpu.CompilerParams(vmem_limit_bytes=mib * 1024 * 1024)


def row_orders(n_z, rows):
    group = -(-n_z * rows // 8) * 8
    grouped = np.full((4 * group, 1), -1, np.int32)
    natural = np.zeros((n_z * 4 * rows, 1), np.int32)
    for z in range(n_z):
        for y in range(2):
            for c in range(2):
                for r in range(rows):
                    o = ((z * 2 + y) * 2 + c) * rows + r
                    p = (c * 2 + y) * group + z * rows + r
                    grouped[p, 0] = o
                    natural[o, 0] = p
    return group, grouped, natural


def pick(index, width):
    lanes = lax.broadcasted_iota(jnp.int32, (index.shape[0], width), 1)
    return jnp.where(lanes == index, 1.0, 0.0).astype(jnp.bfloat16)


def dot(a, b, ca, cb):
    return lax.dot_general(a, b, (((ca,), (cb,)), ((), ())), preferred_element_type=jnp.float32)


def term_kernel(n_x, place, tokens, gain, cot, order, mine, theirs, cot_grouped, inv):
    feats = tokens.shape[1]
    half, group = order.shape[0] // 2, order.shape[0] // 4
    total = jnp.zeros((tokens.shape[0], COL), jnp.float32)
    for f in range(0, feats, COL):
        v = tokens[:, f : f + COL].astype(jnp.float32)
        total = total + v * v
    r = lax.rsqrt(jnp.sum(total, axis=1, keepdims=True) / feats + EPS)
    inv[...] = jnp.broadcast_to(r, inv.shape)
    for c in range(2):
        chosen = pick(order[c * half : (c + 1) * half, :], cot.shape[0])
        cot_grouped[c] = dot(chosen, cot[...], 1, 0).astype(jnp.bfloat16)
    for f in range(0, feats, COL):
        v = tokens[:, f : f + COL].astype(jnp.float32)
        hid = (v * r * gain[:, f : f + COL].astype(jnp.float32)).astype(jnp.bfloat16)
        y, x = divmod(f // COL, n_x)
        for out, c in ((theirs, 1 - place[0]), (mine, place[0])):
            part = dot(cot_grouped[c], hid, 1, 0)
            slot = lax.rem(x + n_x - place[1], n_x)
            out[slot, 2 * y] = part[:group].astype(jnp.bfloat16)
            out[slot, 2 * y + 1] = part[group:].astype(jnp.bfloat16)


def prep_kernel(cot_grouped, cot):
    cot[...] = cot_grouped[...].T


def main_kernel(tokens, gain, cot, inv, back, w, keys, grad, keys_acc, gh, dots):
    i = pl.program_id(0)
    toks, feats = tokens.shape
    n_x = w.shape[3]
    r = inv[:, :1]

    @pl.when(i == 0)
    def _():
        keys_acc[...] = jnp.zeros_like(keys_acc)
        dots[...] = jnp.zeros_like(dots)

    for x in range(n_x):
        at = pl.ds(pl.multiple_of((i * n_x + x) * COL, COL), COL)
        v = tokens[:, at].astype(jnp.float32)
        g = gain[:, at].astype(jnp.float32)
        hid = (v * r * g).astype(jnp.bfloat16)
        weight = jnp.concatenate([w[0, y, c, x] for c in range(2) for y in range(2)], axis=0)
        keys_acc[...] += dot(weight, hid, 1, 1)
        part = dot(cot[...], weight, 1, 0) * g
        gh[:, at] = part
        dots[...] += v * part

    @pl.when(i == pl.num_programs(0) - 1)
    def _():
        keys[...] = dot(back[...], keys_acc[...].astype(jnp.bfloat16), 1, 0).astype(jnp.bfloat16)
        k = r * r * r * (jnp.sum(dots[...], axis=1, keepdims=True) / feats)
        for f in range(0, feats, COL):
            v = tokens[:, f : f + COL].astype(jnp.float32)
            grad[:, f : f + COL] = (r * gh[:, f : f + COL] - v * k).astype(jnp.bfloat16)


def add(values):
    total = values[0].astype(jnp.float32)
    for i in range(1, len(values)):
        total = total + values[i].astype(jnp.float32)
    return total


def together(*values):
    return lax.optimization_barrier(values)


def per_device(tokens, gain, codes, scales, cotangent):
    n_y, n_x, n_z = (lax.axis_size(a) for a in ("y_hi", "x", "z"))
    rows, width = codes.shape
    toks, feats = tokens.shape
    outw = cotangent.shape[1]
    group, grouped, natural = row_orders(n_z, rows)
    place = jnp.stack([lax.axis_index("core"), lax.axis_index("x")]).astype(jnp.int32)
    gain_row = gain.reshape(1, feats)
    cot_t = cotangent.T

    with jax.named_scope("weight_far"):
        scale = jnp.repeat(scales.astype(jnp.float32), width // scales.shape[1], axis=1)
        own = (codes.astype(jnp.float32) * scale).astype(jnp.bfloat16)
        spread = jnp.broadcast_to(own[None], (n_x * n_z, rows, width))
        spread, tokens_after = together(spread, tokens)
        spread = lax.all_to_all(spread, ("x", "z"), split_axis=0, concat_axis=0, tiled=True)
    with jax.named_scope("term"):
        near = jax.ShapeDtypeStruct((n_x, 2 * n_y, group, width), jnp.bfloat16)
        mine, theirs, cot_grouped, inv = pl.pallas_call(
            lambda *refs: term_kernel(n_x, *refs),
            out_shape=(
                near,
                near,
                jax.ShapeDtypeStruct((2, 2 * group, toks), jnp.bfloat16),
                jax.ShapeDtypeStruct((toks, LANE), jnp.float32),
            ),
            in_specs=[SMEM] + [VMEM] * 4,
            out_specs=(VMEM,) * 4,
            compiler_params=params(20),
            cost_estimate=pl.CostEstimate(flops=3 * toks * outw * feats, bytes_accessed=4 * toks * feats, transcendentals=0),
        )(place, tokens_after, gain_row, cot_t, jnp.asarray(grouped))
        cot_grouped = cot_grouped.reshape(4 * group, toks)
    with jax.named_scope("weight_near"):
        came = lax.ppermute(theirs, "core", ((0, 1), (1, 0)))
        pairs = [(mine[s].astype(jnp.float32) + came[s].astype(jnp.float32)).astype(jnp.bfloat16) for s in range(n_x)]
        parts = [pairs[0]]
        for s in range(1, n_x):
            parts.append(lax.ppermute(pairs[s], "x", [(j, (j + s) % n_x) for j in range(n_x)]))
        spread, parts[1], parts[-1] = together(spread, parts[1], parts[-1])
        slab = jnp.pad(spread.reshape(n_x, n_z * rows, width), ((0, 0), (0, group - n_z * rows), (0, 0)))
        w = lax.all_gather(slab, ("y_hi", "y_lo", "core"), axis=0, tiled=False).reshape(n_y, 2, 2, n_x, group, width)
    with jax.named_scope("reduce_x"):
        cot_after, _ = together(cot_grouped, slab)
        cot = pl.pallas_call(
            prep_kernel,
            out_shape=jax.ShapeDtypeStruct((toks, 4 * group), jnp.bfloat16),
            in_specs=[VMEM],
            out_specs=VMEM,
            compiler_params=params(8),
        )(cot_after)
        cot, *parts = together(cot, *parts)
        part = add(parts).astype(jnp.bfloat16)
    with jax.named_scope("reduce_y"):
        part, order = together(part, jnp.asarray(natural))
        parts = lax.all_to_all(part, ("y_hi", "y_lo"), split_axis=0, concat_axis=0, tiled=True)
        back = pick(order, 4 * group)
        parts, back = together(parts, back)
        part = add(parts).astype(jnp.bfloat16)[: n_z * rows].reshape(n_z, rows, width)
    with jax.named_scope("reduce_z"):
        part, back = together(part, back)
        last = lax.all_to_all(part, "z", split_axis=0, concat_axis=0, tiled=True)
    with jax.named_scope("main"):
        whole = lambda *shape: pl.BlockSpec(shape, lambda i: (0,) * len(shape))
        keys_t, grad_tokens = pl.pallas_call(
            main_kernel,
            grid=(n_y,),
            out_shape=(
                jax.ShapeDtypeStruct((outw, toks), jnp.bfloat16),
                jax.ShapeDtypeStruct((toks, feats), jnp.bfloat16),
            ),
            in_specs=[
                whole(toks, feats),
                whole(1, feats),
                whole(toks, 4 * group),
                whole(toks, LANE),
                whole(outw, 4 * group),
                pl.BlockSpec((1, 2, 2, n_x, group, width), lambda i: (i, 0, 0, 0, 0, 0)),
            ],
            out_specs=(whole(outw, toks), whole(toks, feats)),
            scratch_shapes=[
                pltpu.VMEM((4 * group, toks), jnp.float32),
                pltpu.VMEM((toks, feats), jnp.float32),
                pltpu.VMEM((toks, COL), jnp.float32),
            ],
            compiler_params=params(60),
            cost_estimate=pl.CostEstimate(flops=5 * toks * outw * feats, bytes_accessed=10 * toks * feats, transcendentals=0),
        )(tokens, gain_row, cot, inv, back, w)
    with jax.named_scope("finish"):
        last, keys_t = together(last, keys_t)
        grad_weight = jnp.sum(last.astype(jnp.float32), axis=0) / (n_y * n_x * n_z * 4)
    return keys_t.T, grad_tokens, grad_weight


def solution(mesh):
    n_intra, n_inter = mesh.devices.shape
    fine = Mesh(mesh.devices.reshape(4, n_intra // 4, n_inter // 4, 2, 2), ("y_hi", "x", "z", "y_lo", "core"))
    intra, inter = ("y_hi", "x"), ("z", "y_lo", "core")
    placed = (P(intra + inter, None), P(), P(inter, intra), P(inter, intra), P(intra + inter, None))
    return jax.shard_map(
        per_device,
        mesh=fine,
        in_specs=placed,
        out_specs=(P(intra + inter, None), P(intra + inter, None), P(inter, intra)),
        check_vma=False,
    )
```

```python
import numpy as np
import jax
import jax.numpy as jnp
from jax import lax
from jax.experimental import pallas as pl
from jax.experimental.pallas import tpu as pltpu
from jax.sharding import Mesh, PartitionSpec as P

EPS = 1e-05
COL = 256
LANE = 128
VMEM = pl.BlockSpec(memory_space=pltpu.VMEM)
SMEM = pl.BlockSpec(memory_space=pltpu.SMEM)


def params(mib):
    return pltpu.CompilerParams(vmem_limit_bytes=mib * 1024 * 1024)


def row_orders(n_z, rows):
    group = -(-n_z * rows // 8) * 8
    grouped = np.full((4 * group, 1), -1, np.int32)
    natural = np.zeros((n_z * 4 * rows, 1), np.int32)
    for z in range(n_z):
        for y in range(2):
            for c in range(2):
                for r in range(rows):
                    o = ((z * 2 + y) * 2 + c) * rows + r
                    p = (c * 2 + y) * group + z * rows + r
                    grouped[p, 0] = o
                    natural[o, 0] = p
    return group, grouped, natural


def pick(index, width):
    lanes = lax.broadcasted_iota(jnp.int32, (index.shape[0], width), 1)
    return jnp.where(lanes == index, 1.0, 0.0).astype(jnp.bfloat16)


def dot(a, b, ca, cb):
    return lax.dot_general(a, b, (((ca,), (cb,)), ((), ())), preferred_element_type=jnp.float32)


def term_kernel(n_x, place, tokens, gain, cot, order, mine, theirs, cot_grouped, inv):
    feats = tokens.shape[1]
    half, group = order.shape[0] // 2, order.shape[0] // 4
    total = jnp.zeros((tokens.shape[0], COL), jnp.float32)
    for f in range(0, feats, COL):
        v = tokens[:, f : f + COL].astype(jnp.float32)
        total = total + v * v
    r = lax.rsqrt(jnp.sum(total, axis=1, keepdims=True) / feats + EPS)
    inv[...] = jnp.broadcast_to(r, inv.shape)
    for c in range(2):
        chosen = pick(order[c * half : (c + 1) * half, :], cot.shape[0])
        cot_grouped[c] = dot(chosen, cot[...], 1, 0).astype(jnp.bfloat16)
    for f in range(0, feats, COL):
        v = tokens[:, f : f + COL].astype(jnp.float32)
        hid = (v * r * gain[:, f : f + COL].astype(jnp.float32)).astype(jnp.bfloat16)
        y, x = divmod(f // COL, n_x)
        for out, c in ((theirs, 1 - place[0]), (mine, place[0])):
            part = dot(cot_grouped[c], hid, 1, 0)
            out[x, 2 * y] = part[:group].astype(jnp.bfloat16)
            out[x, 2 * y + 1] = part[group:].astype(jnp.bfloat16)


def prep_kernel(cot_grouped, cot):
    cot[...] = cot_grouped[...].T


def keys_kernel(order, grouped, keys):
    keys[...] = dot(pick(order[...], grouped.shape[0]), grouped[...], 1, 0).astype(jnp.bfloat16)


def main_kernel(tokens, gain, cot, inv, w, keys, grad, keys_acc, gh, dots):
    i = pl.program_id(0)
    toks, feats = tokens.shape
    n_x = w.shape[3]
    r = inv[:, :1]

    @pl.when(i == 0)
    def _():
        keys_acc[...] = jnp.zeros_like(keys_acc)
        dots[...] = jnp.zeros_like(dots)

    for x in range(n_x):
        at = pl.ds(pl.multiple_of((i * n_x + x) * COL, COL), COL)
        v = tokens[:, at].astype(jnp.float32)
        g = gain[:, at].astype(jnp.float32)
        hid = (v * r * g).astype(jnp.bfloat16)
        weight = jnp.concatenate([w[0, y, c, x] for c in range(2) for y in range(2)], axis=0)
        keys_acc[...] += dot(weight, hid, 1, 1)
        part = dot(cot[...], weight, 1, 0) * g
        gh[:, at] = part
        dots[...] += v * part

    @pl.when(i == pl.num_programs(0) - 1)
    def _():
        keys[...] = keys_acc[...].astype(jnp.bfloat16)
        k = r * r * r * (jnp.sum(dots[...], axis=1, keepdims=True) / feats)
        for f in range(0, feats, COL):
            v = tokens[:, f : f + COL].astype(jnp.float32)
            grad[:, f : f + COL] = (r * gh[:, f : f + COL] - v * k).astype(jnp.bfloat16)


def add(values):
    total = values[0].astype(jnp.float32)
    for i in range(1, values.shape[0]):
        total = total + values[i].astype(jnp.float32)
    return total


def together(*values):
    return lax.optimization_barrier(values)


def per_device(tokens, gain, codes, scales, cotangent):
    n_y, n_x, n_z = (lax.axis_size(a) for a in ("y_hi", "x", "z"))
    rows, width = codes.shape
    toks, feats = tokens.shape
    outw = cotangent.shape[1]
    group, grouped, natural = row_orders(n_z, rows)
    place = lax.axis_index("core").astype(jnp.int32).reshape(1)
    gain_row = gain.reshape(1, feats)
    cot_t = cotangent.T

    with jax.named_scope("weight_far"):
        scale = jnp.repeat(scales.astype(jnp.float32), width // scales.shape[1], axis=1)
        own = (codes.astype(jnp.float32) * scale).astype(jnp.bfloat16)
        spread = jnp.broadcast_to(own[None], (n_x * n_z, rows, width))
        spread, tokens_after = together(spread, tokens)
        spread = lax.all_to_all(spread, ("x", "z"), split_axis=0, concat_axis=0, tiled=True)
    with jax.named_scope("term"):
        near = jax.ShapeDtypeStruct((n_x, 2 * n_y, group, width), jnp.bfloat16)
        mine, theirs, cot_grouped, inv = pl.pallas_call(
            lambda *refs: term_kernel(n_x, *refs),
            out_shape=(
                near,
                near,
                jax.ShapeDtypeStruct((2, 2 * group, toks), jnp.bfloat16),
                jax.ShapeDtypeStruct((toks, LANE), jnp.float32),
            ),
            in_specs=[SMEM] + [VMEM] * 4,
            out_specs=(VMEM,) * 4,
            compiler_params=params(20),
            cost_estimate=pl.CostEstimate(flops=3 * toks * outw * feats, bytes_accessed=4 * toks * feats, transcendentals=0),
        )(place, tokens_after, gain_row, cot_t, jnp.asarray(grouped))
        cot_grouped = cot_grouped.reshape(4 * group, toks)
    with jax.named_scope("weight_near"):
        came = lax.ppermute(theirs, "core", ((0, 1), (1, 0)))
        pair = (mine.astype(jnp.float32) + came.astype(jnp.float32)).astype(jnp.bfloat16)
        spread, pair = together(spread, pair)
        slab = jnp.pad(spread.reshape(n_x, n_z * rows, width), ((0, 0), (0, group - n_z * rows), (0, 0)))
        w = lax.all_gather(slab, ("y_hi", "y_lo", "core"), axis=0, tiled=False).reshape(n_y, 2, 2, n_x, group, width)
    with jax.named_scope("reduce_x"):
        cot_after, _ = together(cot_grouped, slab)
        parts = lax.all_to_all(pair, "x", split_axis=0, concat_axis=0, tiled=True)
        cot = pl.pallas_call(
            prep_kernel,
            out_shape=jax.ShapeDtypeStruct((toks, 4 * group), jnp.bfloat16),
            in_specs=[VMEM],
            out_specs=VMEM,
            compiler_params=params(8),
        )(cot_after)
        parts, cot = together(parts, cot)
        part = add(parts).astype(jnp.bfloat16)
    with jax.named_scope("reduce_y"):
        part, inv = together(part, inv)
        parts = lax.all_to_all(part, ("y_hi", "y_lo"), split_axis=0, concat_axis=0, tiled=True)
    with jax.named_scope("main"):
        whole = lambda *shape: pl.BlockSpec(shape, lambda i: (0,) * len(shape))
        keys_grouped, grad_tokens = pl.pallas_call(
            main_kernel,
            grid=(n_y,),
            out_shape=(
                jax.ShapeDtypeStruct((4 * group, toks), jnp.bfloat16),
                jax.ShapeDtypeStruct((toks, feats), jnp.bfloat16),
            ),
            in_specs=[
                whole(toks, feats),
                whole(1, feats),
                whole(toks, 4 * group),
                whole(toks, LANE),
                pl.BlockSpec((1, 2, 2, n_x, group, width), lambda i: (i, 0, 0, 0, 0, 0)),
            ],
            out_specs=(whole(4 * group, toks), whole(toks, feats)),
            scratch_shapes=[
                pltpu.VMEM((4 * group, toks), jnp.float32),
                pltpu.VMEM((toks, feats), jnp.float32),
                pltpu.VMEM((toks, COL), jnp.float32),
            ],
            compiler_params=params(60),
            cost_estimate=pl.CostEstimate(flops=5 * toks * outw * feats, bytes_accessed=10 * toks * feats, transcendentals=0),
        )(tokens, gain_row, cot, inv, w)
    with jax.named_scope("reduce_z"):
        parts, grad_tokens = together(parts, grad_tokens)
        part = add(parts).astype(jnp.bfloat16)[: n_z * rows].reshape(n_z, rows, width)
        part, keys_grouped = together(part, keys_grouped)
        last = lax.all_to_all(part, "z", split_axis=0, concat_axis=0, tiled=True)
        keys_t = pl.pallas_call(
            keys_kernel,
            out_shape=jax.ShapeDtypeStruct((outw, toks), jnp.bfloat16),
            in_specs=[VMEM] * 2,
            out_specs=VMEM,
            compiler_params=params(8),
        )(jnp.asarray(natural), keys_grouped)
        last, keys_t = together(last, keys_t)
        grad_weight = jnp.sum(last.astype(jnp.float32), axis=0) / (n_y * n_x * n_z * 4)
    return keys_t.T, grad_tokens, grad_weight


def solution(mesh):
    n_intra, n_inter = mesh.devices.shape
    fine = Mesh(mesh.devices.reshape(4, n_intra // 4, n_inter // 4, 2, 2), ("y_hi", "x", "z", "y_lo", "core"))
    intra, inter = ("y_hi", "x"), ("z", "y_lo", "core")
    placed = (P(intra + inter, None), P(), P(inter, intra), P(inter, intra), P(intra + inter, None))
    return jax.shard_map(
        per_device,
        mesh=fine,
        in_specs=placed,
        out_specs=(P(intra + inter, None), P(intra + inter, None), P(inter, intra)),
        check_vma=False,
    )
```

```python
import numpy as np
import jax
import jax.numpy as jnp
from jax import lax
from jax.experimental import pallas as pl
from jax.experimental.pallas import tpu as pltpu
from jax.sharding import Mesh, PartitionSpec as P

EPS = 1e-05
COL = 256
LANE = 128
VMEM = pl.BlockSpec(memory_space=pltpu.VMEM)
SMEM = pl.BlockSpec(memory_space=pltpu.SMEM)


def params(mib):
    return pltpu.CompilerParams(vmem_limit_bytes=mib * 1024 * 1024)


def row_orders(n_z, rows):
    group = -(-n_z * rows // 8) * 8
    grouped = np.full((4 * group, 1), -1, np.int32)
    natural = np.zeros((n_z * 4 * rows, 1), np.int32)
    for z in range(n_z):
        for y in range(2):
            for c in range(2):
                for r in range(rows):
                    o = ((z * 2 + y) * 2 + c) * rows + r
                    p = (c * 2 + y) * group + z * rows + r
                    grouped[p, 0] = o
                    natural[o, 0] = p
    return group, grouped, natural


def pick(index, width):
    lanes = lax.broadcasted_iota(jnp.int32, (index.shape[0], width), 1)
    return jnp.where(lanes == index, 1.0, 0.0).astype(jnp.bfloat16)


def dot(a, b, ca, cb):
    return lax.dot_general(a, b, (((ca,), (cb,)), ((), ())), preferred_element_type=jnp.float32)


def term_kernel(n_x, place, tokens, gain, cot, order, mine, theirs, cot_grouped, inv):
    feats = tokens.shape[1]
    half, group = order.shape[0] // 2, order.shape[0] // 4
    total = jnp.zeros((tokens.shape[0], COL), jnp.float32)
    for f in range(0, feats, COL):
        v = tokens[:, f : f + COL].astype(jnp.float32)
        total = total + v * v
    r = lax.rsqrt(jnp.sum(total, axis=1, keepdims=True) / feats + EPS)
    inv[...] = jnp.broadcast_to(r, inv.shape)
    for c in range(2):
        chosen = pick(order[c * half : (c + 1) * half, :], cot.shape[0])
        cot_grouped[c] = dot(chosen, cot[...], 1, 0).astype(jnp.bfloat16)
    for f in range(0, feats, COL):
        v = tokens[:, f : f + COL].astype(jnp.float32)
        hid = (v * r * gain[:, f : f + COL].astype(jnp.float32)).astype(jnp.bfloat16)
        y, x = divmod(f // COL, n_x)
        for out, c in ((theirs, 1 - place[0]), (mine, place[0])):
            part = dot(cot_grouped[c], hid, 1, 0)
            out[x, 2 * y] = part[:group].astype(jnp.bfloat16)
            out[x, 2 * y + 1] = part[group:].astype(jnp.bfloat16)


def prep_kernel(cot_grouped, cot):
    cot[...] = cot_grouped[...].T


def main_kernel(tokens, gain, cot, inv, back, w, keys, grad, keys_acc, gh, dots):
    i = pl.program_id(0)
    toks, feats = tokens.shape
    n_x = w.shape[3]
    r = inv[:, :1]

    @pl.when(i == 0)
    def _():
        keys_acc[...] = jnp.zeros_like(keys_acc)
        dots[...] = jnp.zeros_like(dots)

    for x in range(n_x):
        at = pl.ds(pl.multiple_of((i * n_x + x) * COL, COL), COL)
        v = tokens[:, at].astype(jnp.float32)
        g = gain[:, at].astype(jnp.float32)
        hid = (v * r * g).astype(jnp.bfloat16)
        weight = jnp.concatenate([w[0, y, c, x] for c in range(2) for y in range(2)], axis=0)
        keys_acc[...] += dot(weight, hid, 1, 1)
        part = dot(cot[...], weight, 1, 0) * g
        gh[:, at] = part
        dots[...] += v * part

    @pl.when(i == pl.num_programs(0) - 1)
    def _():
        keys[...] = dot(back[...], keys_acc[...].astype(jnp.bfloat16), 1, 0).astype(jnp.bfloat16)
        k = r * r * r * (jnp.sum(dots[...], axis=1, keepdims=True) / feats)
        for f in range(0, feats, COL):
            v = tokens[:, f : f + COL].astype(jnp.float32)
            grad[:, f : f + COL] = (r * gh[:, f : f + COL] - v * k).astype(jnp.bfloat16)


def add(values):
    total = values[0].astype(jnp.float32)
    for i in range(1, values.shape[0]):
        total = total + values[i].astype(jnp.float32)
    return total


def together(*values):
    return lax.optimization_barrier(values)


def per_device(tokens, gain, codes, scales, cotangent):
    n_y, n_x, n_z = (lax.axis_size(a) for a in ("y_hi", "x", "z"))
    rows, width = codes.shape
    toks, feats = tokens.shape
    outw = cotangent.shape[1]
    group, grouped, natural = row_orders(n_z, rows)
    place = lax.axis_index("core").astype(jnp.int32).reshape(1)
    gain_row = gain.reshape(1, feats)
    cot_t = cotangent.T

    with jax.named_scope("weight_far"):
        scale = jnp.repeat(scales.astype(jnp.float32), width // scales.shape[1], axis=1)
        own = (codes.astype(jnp.float32) * scale).astype(jnp.bfloat16)
        spread = jnp.broadcast_to(own[None], (n_z, rows, width))
        spread, tokens_after = together(spread, tokens)
        spread = lax.all_to_all(spread, "z", split_axis=0, concat_axis=0, tiled=True)

    with jax.named_scope("term"):
        near = jax.ShapeDtypeStruct((n_x, 2 * n_y, group, width), jnp.bfloat16)
        mine, theirs, cot_grouped, inv = pl.pallas_call(
            lambda *refs: term_kernel(n_x, *refs),
            out_shape=(
                near,
                near,
                jax.ShapeDtypeStruct((2, 2 * group, toks), jnp.bfloat16),
                jax.ShapeDtypeStruct((toks, LANE), jnp.float32),
            ),
            in_specs=[SMEM] + [VMEM] * 4,
            out_specs=(VMEM,) * 4,
            compiler_params=params(20),
            cost_estimate=pl.CostEstimate(flops=3 * toks * outw * feats, bytes_accessed=4 * toks * feats, transcendentals=0),
        )(place, tokens_after, gain_row, cot_t, jnp.asarray(grouped))
        cot_grouped = cot_grouped.reshape(4 * group, toks)
    with jax.named_scope("weight_x"):
        spread, theirs = together(spread, theirs)
        strip = jnp.pad(spread.reshape(n_z * rows, width), ((0, group - n_z * rows), (0, 0)))
        slab = jnp.broadcast_to(strip[None], (n_x, group, width))
        slab = lax.all_to_all(slab, "x", split_axis=0, concat_axis=0, tiled=True)
    with jax.named_scope("reduce_core"):
        came = lax.ppermute(theirs, "core", ((0, 1), (1, 0)))
        pair = (mine.astype(jnp.float32) + came.astype(jnp.float32)).astype(jnp.bfloat16)
    with jax.named_scope("weight_near"):
        slab, pair = together(slab, pair)
        w = lax.all_gather(slab, ("y_hi", "y_lo", "core"), axis=0, tiled=False).reshape(n_y, 2, 2, n_x, group, width)
    with jax.named_scope("reduce_x"):
        cot_after, _ = together(cot_grouped, slab)
        parts = lax.all_to_all(pair, "x", split_axis=0, concat_axis=0, tiled=True)
        cot = pl.pallas_call(
            prep_kernel,
            out_shape=jax.ShapeDtypeStruct((toks, 4 * group), jnp.bfloat16),
            in_specs=[VMEM],
            out_specs=VMEM,
            compiler_params=params(8),
        )(cot_after)
        parts, cot = together(parts, cot)
        part = add(parts).astype(jnp.bfloat16)
    with jax.named_scope("reduce_y"):
        part, order = together(part, jnp.asarray(natural))
        parts = lax.all_to_all(part, ("y_hi", "y_lo"), split_axis=0, concat_axis=0, tiled=True)
        back = pick(order, 4 * group)
        parts, back = together(parts, back)
        part = add(parts).astype(jnp.bfloat16)[: n_z * rows].reshape(n_z, rows, width)
    with jax.named_scope("reduce_z"):
        part, back = together(part, back)
        last = lax.all_to_all(part, "z", split_axis=0, concat_axis=0, tiled=True)
    with jax.named_scope("main"):
        whole = lambda *shape: pl.BlockSpec(shape, lambda i: (0,) * len(shape))
        keys_t, grad_tokens = pl.pallas_call(
            main_kernel,
            grid=(n_y,),
            out_shape=(
                jax.ShapeDtypeStruct((outw, toks), jnp.bfloat16),
                jax.ShapeDtypeStruct((toks, feats), jnp.bfloat16),
            ),
            in_specs=[
                whole(toks, feats),
                whole(1, feats),
                whole(toks, 4 * group),
                whole(toks, LANE),
                whole(outw, 4 * group),
                pl.BlockSpec((1, 2, 2, n_x, group, width), lambda i: (i, 0, 0, 0, 0, 0)),
            ],
            out_specs=(whole(outw, toks), whole(toks, feats)),
            scratch_shapes=[
                pltpu.VMEM((4 * group, toks), jnp.float32),
                pltpu.VMEM((toks, feats), jnp.float32),
                pltpu.VMEM((toks, COL), jnp.float32),
            ],
            compiler_params=params(60),
            cost_estimate=pl.CostEstimate(flops=5 * toks * outw * feats, bytes_accessed=10 * toks * feats, transcendentals=0),
        )(tokens, gain_row, cot, inv, back, w)
    with jax.named_scope("finish"):
        last, keys_t = together(last, keys_t)
        grad_weight = jnp.sum(last.astype(jnp.float32), axis=0) / (n_y * n_x * n_z * 4)
    return keys_t.T, grad_tokens, grad_weight


def solution(mesh):
    n_intra, n_inter = mesh.devices.shape
    fine = Mesh(mesh.devices.reshape(4, n_intra // 4, n_inter // 4, 2, 2), ("y_hi", "x", "z", "y_lo", "core"))
    intra, inter = ("y_hi", "x"), ("z", "y_lo", "core")
    placed = (P(intra + inter, None), P(), P(inter, intra), P(inter, intra), P(intra + inter, None))
    return jax.shard_map(
        per_device,
        mesh=fine,
        in_specs=placed,
        out_specs=(P(intra + inter, None), P(intra + inter, None), P(inter, intra)),
        check_vma=False,
    )
```

```python
import numpy as np
import jax
import jax.numpy as jnp
from jax import lax
from jax.experimental import pallas as pl
from jax.experimental.pallas import tpu as pltpu
from jax.sharding import Mesh, PartitionSpec as P

EPS = 1e-05
COL = 256
LANE = 128
VMEM = pl.BlockSpec(memory_space=pltpu.VMEM)
SMEM = pl.BlockSpec(memory_space=pltpu.SMEM)


def params(mib):
    return pltpu.CompilerParams(vmem_limit_bytes=mib * 1024 * 1024)


def row_orders(n_z, rows):
    group = -(-n_z * rows // 8) * 8
    grouped = np.full((4 * group, 1), -1, np.int32)
    natural = np.zeros((n_z * 4 * rows, 1), np.int32)
    for z in range(n_z):
        for y in range(2):
            for c in range(2):
                for r in range(rows):
                    o = ((z * 2 + y) * 2 + c) * rows + r
                    p = (c * 2 + y) * group + z * rows + r
                    grouped[p, 0] = o
                    natural[o, 0] = p
    return group, grouped, natural


def pick(index, width):
    lanes = lax.broadcasted_iota(jnp.int32, (index.shape[0], width), 1)
    return jnp.where(lanes == index, 1.0, 0.0).astype(jnp.bfloat16)


def dot(a, b, ca, cb):
    return lax.dot_general(a, b, (((ca,), (cb,)), ((), ())), preferred_element_type=jnp.float32)


def dequantize_kernel(codes, scales, copies):
    n_blocks, width = scales.shape[0], codes.shape[1]
    rows = lax.broadcasted_iota(jnp.int32, (n_blocks, width), 0)
    lanes = lax.broadcasted_iota(jnp.int32, (n_blocks, width), 1) // (width // n_blocks)
    spread = jnp.where(rows == lanes, 1.0, 0.0).astype(jnp.bfloat16)
    weight = codes[...].astype(jnp.float32) * dot(scales[...], spread, 0, 0)
    for z in range(copies.shape[0]):
        copies[z] = weight.astype(jnp.bfloat16)


def term_kernel(n_x, place, tokens, gain, cot, order, mine, theirs, cot_grouped, inv):
    feats = tokens.shape[1]
    half, group = order.shape[0] // 2, order.shape[0] // 4
    total = jnp.zeros((tokens.shape[0], COL), jnp.float32)
    for f in range(0, feats, COL):
        v = tokens[:, f : f + COL].astype(jnp.float32)
        total = total + v * v
    r = lax.rsqrt(jnp.sum(total, axis=1, keepdims=True) / feats + EPS)
    inv[...] = jnp.broadcast_to(r, inv.shape)
    for c in range(2):
        chosen = pick(order[c * half : (c + 1) * half, :], cot.shape[0])
        cot_grouped[c] = dot(chosen, cot[...], 1, 0).astype(jnp.bfloat16)
    for f in range(0, feats, COL):
        v = tokens[:, f : f + COL].astype(jnp.float32)
        hid = (v * r * gain[:, f : f + COL].astype(jnp.float32)).astype(jnp.bfloat16)
        y, x = divmod(f // COL, n_x)
        for out, c in ((theirs, 1 - place[0]), (mine, place[0])):
            part = dot(cot_grouped[c], hid, 1, 0)
            out[x, 2 * y] = part[:group].astype(jnp.bfloat16)
            out[x, 2 * y + 1] = part[group:].astype(jnp.bfloat16)


def prep_kernel(cot_grouped, cot):
    cot[...] = cot_grouped[...].T


def main_kernel(tokens, gain, cot, inv, back, w, keys, grad, keys_acc, gh, dots, held):
    i = pl.program_id(0)
    feats = grad.shape[1]
    n_x = w.shape[3]
    r = inv[:, :1]

    @pl.when(i == 0)
    def _():
        keys_acc[...] = jnp.zeros_like(keys_acc)
        dots[...] = jnp.zeros_like(dots)

    for x in range(n_x):
        at = pl.ds(pl.multiple_of((i * n_x + x) * COL, COL), COL)
        held[:, at] = tokens[:, x * COL : (x + 1) * COL]
        v = tokens[:, x * COL : (x + 1) * COL].astype(jnp.float32)
        g = gain[:, at].astype(jnp.float32)
        hid = (v * r * g).astype(jnp.bfloat16)
        weight = jnp.concatenate([w[0, y, c, x] for c in range(2) for y in range(2)], axis=0)
        keys_acc[...] += dot(weight, hid, 1, 1)
        part = dot(cot[...], weight, 1, 0) * g
        gh[:, at] = part
        dots[...] += v * part

    @pl.when(i == pl.num_programs(0) - 1)
    def _():
        keys[...] = dot(back[...], keys_acc[...].astype(jnp.bfloat16), 1, 0).astype(jnp.bfloat16)
        k = r * r * r * (jnp.sum(dots[...], axis=1, keepdims=True) / feats)
        for f in range(0, feats, COL):
            v = held[:, f : f + COL].astype(jnp.float32)
            grad[:, f : f + COL] = (r * gh[:, f : f + COL] - v * k).astype(jnp.bfloat16)


def add(values):
    total = values[0].astype(jnp.float32)
    for i in range(1, values.shape[0]):
        total = total + values[i].astype(jnp.float32)
    return total


def together(*values):
    return lax.optimization_barrier(values)


def per_device(tokens, gain, codes, scales, cotangent):
    n_y, n_x, n_z = (lax.axis_size(a) for a in ("y_hi", "x", "z"))
    rows, width = codes.shape
    toks, feats = tokens.shape
    outw = cotangent.shape[1]
    group, grouped, natural = row_orders(n_z, rows)
    place = lax.axis_index("core").astype(jnp.int32).reshape(1)
    gain_row = gain.reshape(1, feats)
    cot_t = cotangent.T

    with jax.named_scope("weight_far"):
        spread = pl.pallas_call(
            dequantize_kernel,
            out_shape=jax.ShapeDtypeStruct((n_z, rows, width), jnp.bfloat16),
            in_specs=[VMEM] * 2,
            out_specs=VMEM,
            compiler_params=params(8),
        )(codes, scales.T)
        spread, place = together(spread, place)
        spread = lax.all_to_all(spread, "z", split_axis=0, concat_axis=0, tiled=True)

    with jax.named_scope("term"):
        near = jax.ShapeDtypeStruct((n_x, 2 * n_y, group, width), jnp.bfloat16)
        mine, theirs, cot_grouped, inv = pl.pallas_call(
            lambda *refs: term_kernel(n_x, *refs),
            out_shape=(
                near,
                near,
                jax.ShapeDtypeStruct((2, 2 * group, toks), jnp.bfloat16),
                jax.ShapeDtypeStruct((toks, LANE), jnp.float32),
            ),
            in_specs=[SMEM] + [VMEM] * 4,
            out_specs=(VMEM,) * 4,
            compiler_params=params(20),
            cost_estimate=pl.CostEstimate(flops=3 * toks * outw * feats, bytes_accessed=4 * toks * feats, transcendentals=0),
        )(place, tokens, gain_row, cot_t, jnp.asarray(grouped))
        cot_grouped = cot_grouped.reshape(4 * group, toks)
    with jax.named_scope("weight_x"):
        spread, theirs = together(spread, theirs)
        strip = jnp.pad(spread.reshape(n_z * rows, width), ((0, group - n_z * rows), (0, 0)))
        slab = jnp.broadcast_to(strip[None], (n_x, group, width))
        slab = lax.all_to_all(slab, "x", split_axis=0, concat_axis=0, tiled=True)
    with jax.named_scope("reduce_core"):
        came = lax.ppermute(theirs, "core", ((0, 1), (1, 0)))
        pair = (mine.astype(jnp.float32) + came.astype(jnp.float32)).astype(jnp.bfloat16)
    with jax.named_scope("weight_near"):
        slab, pair = together(slab, pair)
        w = lax.all_gather(slab, ("y_hi", "y_lo", "core"), axis=0, tiled=False).reshape(n_y, 2, 2, n_x, group, width)
    with jax.named_scope("reduce_x"):
        cot_after, _ = together(cot_grouped, slab)
        parts = lax.all_to_all(pair, "x", split_axis=0, concat_axis=0, tiled=True)
        cot = pl.pallas_call(
            prep_kernel,
            out_shape=jax.ShapeDtypeStruct((toks, 4 * group), jnp.bfloat16),
            in_specs=[VMEM],
            out_specs=VMEM,
            compiler_params=params(8),
        )(cot_after)
        parts, cot = together(parts, cot)
        part = add(parts).astype(jnp.bfloat16)
    with jax.named_scope("reduce_y"):
        part, order = together(part, jnp.asarray(natural))
        parts = lax.all_to_all(part, ("y_hi", "y_lo"), split_axis=0, concat_axis=0, tiled=True)
        back = pick(order, 4 * group)
        parts, back = together(parts, back)
        part = add(parts).astype(jnp.bfloat16)[: n_z * rows].reshape(n_z, rows, width)
    with jax.named_scope("reduce_z"):
        part, back = together(part, back)
        last = lax.all_to_all(part, "z", split_axis=0, concat_axis=0, tiled=True)
    with jax.named_scope("main"):
        whole = lambda *shape: pl.BlockSpec(shape, lambda i: (0,) * len(shape))
        keys_t, grad_tokens = pl.pallas_call(
            main_kernel,
            grid=(n_y,),
            out_shape=(
                jax.ShapeDtypeStruct((outw, toks), jnp.bfloat16),
                jax.ShapeDtypeStruct((toks, feats), jnp.bfloat16),
            ),
            in_specs=[
                pl.BlockSpec((toks, n_x * width), lambda i: (0, i)),
                whole(1, feats),
                whole(toks, 4 * group),
                whole(toks, LANE),
                whole(outw, 4 * group),
                pl.BlockSpec((1, 2, 2, n_x, group, width), lambda i: (i, 0, 0, 0, 0, 0)),
            ],
            out_specs=(whole(outw, toks), whole(toks, feats)),
            scratch_shapes=[
                pltpu.VMEM((4 * group, toks), jnp.float32),
                pltpu.VMEM((toks, feats), jnp.float32),
                pltpu.VMEM((toks, COL), jnp.float32),
                pltpu.VMEM((toks, feats), jnp.bfloat16),
            ],
            compiler_params=params(60),
            cost_estimate=pl.CostEstimate(flops=5 * toks * outw * feats, bytes_accessed=10 * toks * feats, transcendentals=0),
        )(tokens, gain_row, cot, inv, back, w)
    with jax.named_scope("finish"):
        last, keys_t = together(last, keys_t)
        grad_weight = jnp.sum(last.astype(jnp.float32), axis=0) / (n_y * n_x * n_z * 4)
    return keys_t.T, grad_tokens, grad_weight


def solution(mesh):
    n_intra, n_inter = mesh.devices.shape
    fine = Mesh(mesh.devices.reshape(4, n_intra // 4, n_inter // 4, 2, 2), ("y_hi", "x", "z", "y_lo", "core"))
    intra, inter = ("y_hi", "x"), ("z", "y_lo", "core")
    placed = (P(intra + inter, None), P(), P(inter, intra), P(inter, intra), P(intra + inter, None))
    return jax.shard_map(
        per_device,
        mesh=fine,
        in_specs=placed,
        out_specs=(P(intra + inter, None), P(intra + inter, None), P(inter, intra)),
        check_vma=False,
    )
```

```python
import numpy as np
import jax
import jax.numpy as jnp
from jax import lax
from jax.experimental import pallas as pl
from jax.experimental.pallas import tpu as pltpu
from jax.sharding import Mesh, PartitionSpec as P

EPS = 1e-05
COL = 256
LANE = 128
VMEM = pl.BlockSpec(memory_space=pltpu.VMEM)
SMEM = pl.BlockSpec(memory_space=pltpu.SMEM)


def params(mib):
    return pltpu.CompilerParams(vmem_limit_bytes=mib * 1024 * 1024)


def row_orders(n_z, rows):
    group = -(-n_z * rows // 8) * 8
    grouped = np.full((4 * group, 1), -1, np.int32)
    natural = np.zeros((n_z * 4 * rows, 1), np.int32)
    for z in range(n_z):
        for y in range(2):
            for c in range(2):
                for r in range(rows):
                    o = ((z * 2 + y) * 2 + c) * rows + r
                    p = (c * 2 + y) * group + z * rows + r
                    grouped[p, 0] = o
                    natural[o, 0] = p
    return group, grouped, natural


def pick(index, width):
    lanes = lax.broadcasted_iota(jnp.int32, (index.shape[0], width), 1)
    return jnp.where(lanes == index, 1.0, 0.0).astype(jnp.bfloat16)


def dot(a, b, ca, cb):
    return lax.dot_general(a, b, (((ca,), (cb,)), ((), ())), preferred_element_type=jnp.float32)


def term_kernel(n_x, place, tokens, gain, cot, order, mine, theirs, cot_grouped, inv):
    feats = tokens.shape[1]
    half, group = order.shape[0] // 2, order.shape[0] // 4
    total = jnp.zeros((tokens.shape[0], COL), jnp.float32)
    for f in range(0, feats, COL):
        v = tokens[:, f : f + COL].astype(jnp.float32)
        total = total + v * v
    r = lax.rsqrt(jnp.sum(total, axis=1, keepdims=True) / feats + EPS)
    inv[...] = jnp.broadcast_to(r, inv.shape)
    for c in range(2):
        chosen = pick(order[c * half : (c + 1) * half, :], cot.shape[0])
        cot_grouped[c] = dot(chosen, cot[...], 1, 0).astype(jnp.bfloat16)
    for f in range(0, feats, COL):
        v = tokens[:, f : f + COL].astype(jnp.float32)
        hid = (v * r * gain[:, f : f + COL].astype(jnp.float32)).astype(jnp.bfloat16)
        y, x = divmod(f // COL, n_x)
        for out, c in ((theirs, 1 - place[0]), (mine, place[0])):
            part = dot(cot_grouped[c], hid, 1, 0)
            out[x, 2 * y] = part[:group].astype(jnp.bfloat16)
            out[x, 2 * y + 1] = part[group:].astype(jnp.bfloat16)


def prep_kernel(cot_grouped, order, cot, move):
    cot[...] = cot_grouped[...].T
    move[...] = pick(order[...], move.shape[1])


def sum_kernel(parts, move, out):
    total = parts[0].astype(jnp.float32)
    for i in range(1, parts.shape[0]):
        total = total + parts[i].astype(jnp.float32)
    out[...] = dot(move[...], total.astype(jnp.bfloat16), 1, 0).astype(jnp.bfloat16)


def keys_kernel(order, grouped, keys):
    keys[...] = dot(pick(order[...], grouped.shape[0]), grouped[...], 1, 0).astype(jnp.bfloat16)


def main_kernel(tokens, gain, cot, inv, w, keys, grad, keys_acc, gh, dots):
    i = pl.program_id(0)
    toks, feats = tokens.shape
    n_x = w.shape[3]
    r = inv[:, :1]

    @pl.when(i == 0)
    def _():
        keys_acc[...] = jnp.zeros_like(keys_acc)
        dots[...] = jnp.zeros_like(dots)

    for x in range(n_x):
        at = pl.ds(pl.multiple_of((i * n_x + x) * COL, COL), COL)
        v = tokens[:, at].astype(jnp.float32)
        g = gain[:, at].astype(jnp.float32)
        hid = (v * r * g).astype(jnp.bfloat16)
        weight = jnp.concatenate([w[0, y, c, x] for c in range(2) for y in range(2)], axis=0)
        keys_acc[...] += dot(weight, hid, 1, 1)
        part = dot(cot[...], weight, 1, 0) * g
        gh[:, at] = part
        dots[...] += v * part

    @pl.when(i == pl.num_programs(0) - 1)
    def _():
        keys[...] = keys_acc[...].astype(jnp.bfloat16)
        k = r * r * r * (jnp.sum(dots[...], axis=1, keepdims=True) / feats)
        for f in range(0, feats, COL):
            v = tokens[:, f : f + COL].astype(jnp.float32)
            grad[:, f : f + COL] = (r * gh[:, f : f + COL] - v * k).astype(jnp.bfloat16)


def add(values):
    total = values[0].astype(jnp.float32)
    for i in range(1, values.shape[0]):
        total = total + values[i].astype(jnp.float32)
    return total


def together(*values):
    return lax.optimization_barrier(values)


def per_device(tokens, gain, codes, scales, cotangent):
    n_y, n_x, n_z = (lax.axis_size(a) for a in ("y_hi", "x", "z"))
    rows, width = codes.shape
    toks, feats = tokens.shape
    outw = cotangent.shape[1]
    group, grouped, natural = row_orders(n_z, rows)
    by_z = np.arange(2 * n_y)[None, :, None] * group + np.arange(n_z * rows).reshape(n_z, 1, rows)
    by_z = by_z.reshape(-1, 1).astype(np.int32)
    move_shape = (by_z.shape[0], 2 * n_y * group)
    place = lax.axis_index("core").astype(jnp.int32).reshape(1)
    gain_row = gain.reshape(1, feats)
    cot_t = cotangent.T

    with jax.named_scope("weight_far"):
        scale = jnp.repeat(scales.astype(jnp.float32), width // scales.shape[1], axis=1)
        own = (codes.astype(jnp.float32) * scale).astype(jnp.bfloat16)
        spread = jnp.broadcast_to(own[None], (n_z, rows, width))
        spread, tokens_after = together(spread, tokens)
        spread = lax.all_to_all(spread, "z", split_axis=0, concat_axis=0, tiled=True)

    with jax.named_scope("term"):
        near = jax.ShapeDtypeStruct((n_x, 2 * n_y, group, width), jnp.bfloat16)
        mine, theirs, cot_grouped, inv = pl.pallas_call(
            lambda *refs: term_kernel(n_x, *refs),
            out_shape=(
                near,
                near,
                jax.ShapeDtypeStruct((2, 2 * group, toks), jnp.bfloat16),
                jax.ShapeDtypeStruct((toks, LANE), jnp.float32),
            ),
            in_specs=[SMEM] + [VMEM] * 4,
            out_specs=(VMEM,) * 4,
            compiler_params=params(20),
            cost_estimate=pl.CostEstimate(flops=3 * toks * outw * feats, bytes_accessed=4 * toks * feats, transcendentals=0),
        )(place, tokens_after, gain_row, cot_t, jnp.asarray(grouped))
        cot_grouped = cot_grouped.reshape(4 * group, toks)
    with jax.named_scope("weight_x"):
        spread, theirs = together(spread, theirs)
        strip = jnp.pad(spread.reshape(n_z * rows, width), ((0, group - n_z * rows), (0, 0)))
        slab = jnp.broadcast_to(strip[None], (n_x, group, width))
        slab = lax.all_to_all(slab, "x", split_axis=0, concat_axis=0, tiled=True)
    with jax.named_scope("reduce_core"):
        came = lax.ppermute(theirs, "core", ((0, 1), (1, 0)))
        pair = (mine.astype(jnp.float32) + came.astype(jnp.float32)).astype(jnp.bfloat16)
    with jax.named_scope("weight_near"):
        slab, pair = together(slab, pair)
        w = lax.all_gather(slab, ("y_hi", "y_lo", "core"), axis=0, tiled=False).reshape(n_y, 2, 2, n_x, group, width)
    with jax.named_scope("reduce_x"):
        cot_after, _ = together(cot_grouped, slab)
        parts = lax.all_to_all(pair, "x", split_axis=0, concat_axis=0, tiled=True)
        cot, move = pl.pallas_call(
            prep_kernel,
            out_shape=(
                jax.ShapeDtypeStruct((toks, 4 * group), jnp.bfloat16),
                jax.ShapeDtypeStruct(move_shape, jnp.bfloat16),
            ),
            in_specs=[VMEM] * 2,
            out_specs=(VMEM,) * 2,
            compiler_params=params(16),
        )(cot_after, jnp.asarray(by_z))
        parts, cot, move = together(parts, cot, move)
        part = pl.pallas_call(
            sum_kernel,
            out_shape=jax.ShapeDtypeStruct((move_shape[0], width), jnp.bfloat16),
            in_specs=[VMEM] * 2,
            out_specs=VMEM,
            compiler_params=params(16),
        )(parts.reshape(n_x, move_shape[1], width), move)
    with jax.named_scope("reduce_z"):
        part, inv = together(part.reshape(n_z, 2 * n_y * rows, width), inv)
        parts = lax.all_to_all(part, "z", split_axis=0, concat_axis=0, tiled=True)
    with jax.named_scope("main"):
        whole = lambda *shape: pl.BlockSpec(shape, lambda i: (0,) * len(shape))
        keys_grouped, grad_tokens = pl.pallas_call(
            main_kernel,
            grid=(n_y,),
            out_shape=(
                jax.ShapeDtypeStruct((4 * group, toks), jnp.bfloat16),
                jax.ShapeDtypeStruct((toks, feats), jnp.bfloat16),
            ),
            in_specs=[
                whole(toks, feats),
                whole(1, feats),
                whole(toks, 4 * group),
                whole(toks, LANE),
                pl.BlockSpec((1, 2, 2, n_x, group, width), lambda i: (i, 0, 0, 0, 0, 0)),
            ],
            out_specs=(whole(4 * group, toks), whole(toks, feats)),
            scratch_shapes=[
                pltpu.VMEM((4 * group, toks), jnp.float32),
                pltpu.VMEM((toks, feats), jnp.float32),
                pltpu.VMEM((toks, COL), jnp.float32),
            ],
            compiler_params=params(60),
            cost_estimate=pl.CostEstimate(flops=5 * toks * outw * feats, bytes_accessed=10 * toks * feats, transcendentals=0),
        )(tokens, gain_row, cot, inv, w)
    with jax.named_scope("reduce_y"):
        parts, grad_tokens = together(parts, grad_tokens)
        part = add(parts).astype(jnp.bfloat16).reshape(2 * n_y, rows, width)
        part, keys_grouped = together(part, keys_grouped)
        last = lax.all_to_all(part, ("y_hi", "y_lo"), split_axis=0, concat_axis=0, tiled=True)
        keys_t = pl.pallas_call(
            keys_kernel,
            out_shape=jax.ShapeDtypeStruct((outw, toks), jnp.bfloat16),
            in_specs=[VMEM] * 2,
            out_specs=VMEM,
            compiler_params=params(8),
        )(jnp.asarray(natural), keys_grouped)
        last, keys_t = together(last, keys_t)
        grad_weight = jnp.sum(last.astype(jnp.float32), axis=0) / (n_y * n_x * n_z * 4)
    return keys_t.T, grad_tokens, grad_weight


def solution(mesh):
    n_intra, n_inter = mesh.devices.shape
    fine = Mesh(mesh.devices.reshape(4, n_intra // 4, n_inter // 4, 2, 2), ("y_hi", "x", "z", "y_lo", "core"))
    intra, inter = ("y_hi", "x"), ("z", "y_lo", "core")
    placed = (P(intra + inter, None), P(), P(inter, intra), P(inter, intra), P(intra + inter, None))
    return jax.shard_map(
        per_device,
        mesh=fine,
        in_specs=placed,
        out_specs=(P(intra + inter, None), P(intra + inter, None), P(inter, intra)),
        check_vma=False,
    )
```

```python
import numpy as np
import jax
import jax.numpy as jnp
from jax import lax
from jax.experimental import pallas as pl
from jax.experimental.pallas import tpu as pltpu
from jax.sharding import Mesh, PartitionSpec as P

EPS = 1e-05
COL = 256
LANE = 128
VMEM = pl.BlockSpec(memory_space=pltpu.VMEM)
SMEM = pl.BlockSpec(memory_space=pltpu.SMEM)


def params(mib):
    return pltpu.CompilerParams(vmem_limit_bytes=mib * 1024 * 1024)


def row_orders(n_z, rows):
    group = -(-n_z * rows // 8) * 8
    grouped = np.full((4 * group, 1), -1, np.int32)
    natural = np.zeros((n_z * 4 * rows, 1), np.int32)
    for z in range(n_z):
        for y in range(2):
            for c in range(2):
                for r in range(rows):
                    o = ((z * 2 + y) * 2 + c) * rows + r
                    p = (c * 2 + y) * group + z * rows + r
                    grouped[p, 0] = o
                    natural[o, 0] = p
    return group, grouped, natural


def pick(index, width):
    lanes = lax.broadcasted_iota(jnp.int32, (index.shape[0], width), 1)
    return jnp.where(lanes == index, 1.0, 0.0).astype(jnp.bfloat16)


def dot(a, b, ca, cb):
    return lax.dot_general(a, b, (((ca,), (cb,)), ((), ())), preferred_element_type=jnp.float32)


def term_kernel(n_x, place, tokens, gain, cot, order, mine, theirs, cot_grouped, inv):
    feats = tokens.shape[1]
    half, group = order.shape[0] // 2, order.shape[0] // 4
    total = jnp.zeros((tokens.shape[0], COL), jnp.float32)
    for f in range(0, feats, COL):
        v = tokens[:, f : f + COL].astype(jnp.float32)
        total = total + v * v
    r = lax.rsqrt(jnp.sum(total, axis=1, keepdims=True) / feats + EPS)
    inv[...] = jnp.broadcast_to(r, inv.shape)
    for c in range(2):
        chosen = pick(order[c * half : (c + 1) * half, :], cot.shape[0])
        cot_grouped[c] = dot(chosen, cot[...], 1, 0).astype(jnp.bfloat16)
    for f in range(0, feats, COL):
        v = tokens[:, f : f + COL].astype(jnp.float32)
        hid = (v * r * gain[:, f : f + COL].astype(jnp.float32)).astype(jnp.bfloat16)
        y, x = divmod(f // COL, n_x)
        for out, c in ((theirs, 1 - place[0]), (mine, place[0])):
            part = dot(cot_grouped[c], hid, 1, 0)
            out[x, 2 * y] = part[:group].astype(jnp.bfloat16)
            out[x, 2 * y + 1] = part[group:].astype(jnp.bfloat16)


def prep_kernel(cot_grouped, cot):
    cot[...] = cot_grouped[...].T


def keys_kernel(order, grouped, keys):
    keys[...] = dot(pick(order[...], grouped.shape[0]), grouped[...], 1, 0).astype(jnp.bfloat16)


def main_kernel(tokens, gain, cot, inv, w, keys, grad, keys_acc, gh, dots):
    i = pl.program_id(0)
    toks, feats = tokens.shape
    n_x = w.shape[3]
    r = inv[:, :1]

    @pl.when(i == 0)
    def _():
        keys_acc[...] = jnp.zeros_like(keys_acc)
        dots[...] = jnp.zeros_like(dots)

    for x in range(n_x):
        at = pl.ds(pl.multiple_of((i * n_x + x) * COL, COL), COL)
        v = tokens[:, at].astype(jnp.float32)
        g = gain[:, at].astype(jnp.float32)
        hid = (v * r * g).astype(jnp.bfloat16)
        weight = jnp.concatenate([w[0, y, c, x] for c in range(2) for y in range(2)], axis=0)
        keys_acc[...] += dot(weight, hid, 1, 1)
        part = dot(cot[...], weight, 1, 0) * g
        gh[:, at] = part
        dots[...] += v * part

    @pl.when(i == pl.num_programs(0) - 1)
    def _():
        keys[...] = keys_acc[...].astype(jnp.bfloat16)
        k = r * r * r * (jnp.sum(dots[...], axis=1, keepdims=True) / feats)
        for f in range(0, feats, COL):
            v = tokens[:, f : f + COL].astype(jnp.float32)
            grad[:, f : f + COL] = (r * gh[:, f : f + COL] - v * k).astype(jnp.bfloat16)


def add(values):
    total = values[0].astype(jnp.float32)
    for i in range(1, values.shape[0]):
        total = total + values[i].astype(jnp.float32)
    return total


def together(*values):
    return lax.optimization_barrier(values)


def per_device(tokens, gain, codes, scales, cotangent):
    n_y, n_x, n_z = (lax.axis_size(a) for a in ("y_hi", "x", "z"))
    rows, width = codes.shape
    toks, feats = tokens.shape
    outw = cotangent.shape[1]
    group, grouped, natural = row_orders(n_z, rows)
    place = lax.axis_index("core").astype(jnp.int32).reshape(1)
    gain_row = gain.reshape(1, feats)
    cot_t = cotangent.T

    with jax.named_scope("weight_far"):
        scale = jnp.repeat(scales.astype(jnp.float32), width // scales.shape[1], axis=1)
        own = (codes.astype(jnp.float32) * scale).astype(jnp.bfloat16)
        spread = jnp.broadcast_to(own[None], (n_z, rows, width))
        spread, tokens_after = together(spread, tokens)
        spread = lax.all_to_all(spread, "z", split_axis=0, concat_axis=0, tiled=True)

    with jax.named_scope("term"):
        near = jax.ShapeDtypeStruct((n_x, 2 * n_y, group, width), jnp.bfloat16)
        mine, theirs, cot_grouped, inv = pl.pallas_call(
            lambda *refs: term_kernel(n_x, *refs),
            out_shape=(
                near,
                near,
                jax.ShapeDtypeStruct((2, 2 * group, toks), jnp.bfloat16),
                jax.ShapeDtypeStruct((toks, LANE), jnp.float32),
            ),
            in_specs=[SMEM] + [VMEM] * 4,
            out_specs=(VMEM,) * 4,
            compiler_params=params(20),
            cost_estimate=pl.CostEstimate(flops=3 * toks * outw * feats, bytes_accessed=4 * toks * feats, transcendentals=0),
        )(place, tokens_after, gain_row, cot_t, jnp.asarray(grouped))
        cot_grouped = cot_grouped.reshape(4 * group, toks)
    with jax.named_scope("weight_x"):
        spread, theirs = together(spread, theirs)
        strip = jnp.pad(spread.reshape(n_z * rows, width), ((0, group - n_z * rows), (0, 0)))
        slab = jnp.broadcast_to(strip[None], (n_x, group, width))
        slab = lax.all_to_all(slab, "x", split_axis=0, concat_axis=0, tiled=True)
    with jax.named_scope("reduce_core"):
        came = lax.ppermute(theirs, "core", ((0, 1), (1, 0)))
        pair = (mine.astype(jnp.float32) + came.astype(jnp.float32)).astype(jnp.bfloat16)
    with jax.named_scope("weight_near"):
        slab, pair = together(slab, pair)
        w = lax.all_gather(slab, ("y_hi", "y_lo", "core"), axis=0, tiled=False).reshape(n_y, 2, 2, n_x, group, width)
    with jax.named_scope("reduce_x"):
        cot_after, _ = together(cot_grouped, slab)
        parts = lax.all_to_all(pair, "x", split_axis=0, concat_axis=0, tiled=True)
        cot = pl.pallas_call(
            prep_kernel,
            out_shape=jax.ShapeDtypeStruct((toks, 4 * group), jnp.bfloat16),
            in_specs=[VMEM],
            out_specs=VMEM,
            compiler_params=params(8),
        )(cot_after)
        parts, cot = together(parts, cot)
        part = add(parts).astype(jnp.bfloat16)
    with jax.named_scope("reduce_y"):
        part, inv = together(part, inv)
        parts = lax.all_to_all(part, ("y_hi", "y_lo"), split_axis=0, concat_axis=0, tiled=True)
    with jax.named_scope("main"):
        whole = lambda *shape: pl.BlockSpec(shape, lambda i: (0,) * len(shape))
        keys_grouped, grad_tokens = pl.pallas_call(
            main_kernel,
            grid=(n_y,),
            out_shape=(
                jax.ShapeDtypeStruct((4 * group, toks), jnp.bfloat16),
                jax.ShapeDtypeStruct((toks, feats), jnp.bfloat16),
            ),
            in_specs=[
                whole(toks, feats),
                whole(1, feats),
                whole(toks, 4 * group),
                whole(toks, LANE),
                pl.BlockSpec((1, 2, 2, n_x, group, width), lambda i: (i, 0, 0, 0, 0, 0)),
            ],
            out_specs=(whole(4 * group, toks), whole(toks, feats)),
            scratch_shapes=[
                pltpu.VMEM((4 * group, toks), jnp.float32),
                pltpu.VMEM((toks, feats), jnp.float32),
                pltpu.VMEM((toks, COL), jnp.float32),
            ],
            compiler_params=params(60),
            cost_estimate=pl.CostEstimate(flops=5 * toks * outw * feats, bytes_accessed=10 * toks * feats, transcendentals=0),
        )(tokens, gain_row, cot, inv, w)
    with jax.named_scope("reduce_z"):
        parts, grad_tokens = together(parts, grad_tokens)
        part = add(parts).astype(jnp.bfloat16)[: n_z * rows].reshape(n_z, rows, width)
        part, keys_grouped = together(part, keys_grouped)
        last = lax.all_to_all(part, "z", split_axis=0, concat_axis=0, tiled=True)
        keys_t = pl.pallas_call(
            keys_kernel,
            out_shape=jax.ShapeDtypeStruct((outw, toks), jnp.bfloat16),
            in_specs=[VMEM] * 2,
            out_specs=VMEM,
            compiler_params=params(8),
        )(jnp.asarray(natural), keys_grouped)
        last, keys_t = together(last, keys_t)
        grad_weight = jnp.sum(last.astype(jnp.float32), axis=0) / (n_y * n_x * n_z * 4)
    return keys_t.T, grad_tokens, grad_weight


def solution(mesh):
    n_intra, n_inter = mesh.devices.shape
    fine = Mesh(mesh.devices.reshape(4, n_intra // 4, n_inter // 4, 2, 2), ("y_hi", "x", "z", "y_lo", "core"))
    intra, inter = ("y_hi", "x"), ("z", "y_lo", "core")
    placed = (P(intra + inter, None), P(), P(inter, intra), P(inter, intra), P(intra + inter, None))
    return jax.shard_map(
        per_device,
        mesh=fine,
        in_specs=placed,
        out_specs=(P(intra + inter, None), P(intra + inter, None), P(inter, intra)),
        check_vma=False,
    )
```
